32 devices in a mesh: ctx: 8 (over y, x, core), head: 4 (over z).
Axes of the slice: x: 2, y: 2, z: 4, core: 2. Of those that a mesh axis runs over, the one named last changes fastest.
Arguments:
- query_vecs: bfloat16 [2048, 4096], P('ctx', 'head'), may hold values from -16 to 16
- key_vecs: bfloat16 [2048, 4096], P('ctx', 'head'), may hold values from -16 to 16
- value_vecs: bfloat16 [2048, 4096], P('ctx', 'head'), may hold values from -9 to 9
- out_grad: bfloat16 [2048, 4096], P('ctx', 'head'), may hold values from -9 to 9
- block_mask: int32 [32, 4], P('ctx'), may hold values from -1 to 31, as said below
- norm_gain: float32 [32, 128], P('head'), may hold values from 0.25 to 1.75
Outputs:
- normed: bfloat16 [2048, 4096], P('ctx', 'head')
- query_grad: bfloat16 [2048, 4096], P('ctx', 'head')
- key_grad: bfloat16 [2048, 4096], P('ctx', 'head')
- value_grad: bfloat16 [2048, 4096], P('ctx', 'head')
- gain_grad: float32 [32, 128], P('head')
The draws below stay inside these ranges and needn't reach their ends.
Inputs may be any that keep to these rules, and one draw needn't show every extreme that they name: `block_mask`: entry 0 of row b is b; every other entry is -1 (no block) or a block index within 2 of b, and the indices of one row are distinct.
All inputs are finite; a program needn't handle non-finite values.
Results may differ from the reference program's by a relative error of at most 0.0073.
Values may be sent and summed in bfloat16 or wider, within the bound.
A program may use at most 128 MiB of HBM per device.

```python
import math
import jax
import jax.numpy as jnp
from jax import lax

HEADS = 32
HEAD_FEATURES = 128
BLOCK = 64
BAND = 2
SLOTS = 4
WIDTH = 4096
SEQUENCE_LENGTH = 2048
NBLOCKS = 32


def pair_draw(key):
    inner_key = jax.random.fold_in(key, 11)
    key_first, key_second = jax.random.split(inner_key, 2)
    dims_all = (SEQUENCE_LENGTH, WIDTH)
    query_part = jax.random.truncated_normal(key_first, -6.0, 6.0, dims_all, jnp.float32)
    key_part = jax.random.truncated_normal(key_second, -6.0, 6.0, dims_all, jnp.float32)
    return (query_part, key_part)


def draw_query_vecs(key, part):
    return pair_draw(key)[0].astype(jnp.bfloat16)


def draw_key_vecs(key, part):
    return pair_draw(key)[1].astype(jnp.bfloat16)


def draw_value_vecs(key, part):
    inner_key = jax.random.fold_in(key, 23)
    dims_all = (SEQUENCE_LENGTH, WIDTH)
    head_of = (jnp.arange(WIDTH) // HEAD_FEATURES).astype(jnp.float32) / (HEADS - 1)
    factor = 0.5 + head_of
    values_raw = jax.random.truncated_normal(inner_key, -6.0, 6.0, dims_all, jnp.float32)
    return (values_raw * factor[None, :]).astype(jnp.bfloat16)


def draw_out_grad(key, part):
    inner_key = jax.random.fold_in(key, 37)
    key_first = jax.random.fold_in(inner_key, 0)
    dims_all = (SEQUENCE_LENGTH, WIDTH)
    along = jnp.arange(SEQUENCE_LENGTH).astype(jnp.float32) / (SEQUENCE_LENGTH - 1)
    factor = 0.5 + along
    grads_raw = jax.random.truncated_normal(key_first, -6.0, 6.0, dims_all, jnp.float32) * factor[:, None]
    return grads_raw.astype(jnp.bfloat16)


def draw_block_mask(key, part):
    inner_key = jax.random.fold_in(key, 29)
    key_first, key_second = jax.random.split(inner_key)
    row_ids = jnp.arange(NBLOCKS)
    logit_scores = jax.random.randint(key_first, (NBLOCKS, 2 * BAND), 0, 1048576) * (2 * BAND) + jnp.arange(2 * BAND)[None, :]
    ranked = jnp.argsort(logit_scores, axis=1, stable=True)[:, :SLOTS - 1]
    offsets = jnp.where(ranked < BAND, ranked - BAND, ranked - BAND + 1)
    target = row_ids[:, None] + offsets
    retained = jax.random.randint(key_second, (NBLOCKS, SLOTS - 1), 0, 4) != 0
    retained = retained & (target >= 0) & (target < NBLOCKS)
    retained = retained.at[0, SLOTS - 2].set(False)
    listed = jnp.where(retained, target, -1)
    return jnp.concatenate([row_ids[:, None], listed], axis=1).astype(jnp.int32)


def setup_inputs(seed: int = 0) -> dict:
    key_list = jax.random.split(jax.random.key(seed), 7)
    return {
        "query_vecs": draw_query_vecs(jax.random.fold_in(key_list[6], 71), 0),
        "key_vecs": draw_key_vecs(jax.random.fold_in(key_list[6], 71), 0),
        "value_vecs": draw_value_vecs(jax.random.fold_in(key_list[6], 71), 0),
        "out_grad": draw_out_grad(jax.random.fold_in(key_list[6], 71), 0),
        "block_mask": draw_block_mask(jax.random.fold_in(key_list[6], 71), 0),
        "norm_gain": jnp.clip(1.0 + 0.15 * jax.random.normal(key_list[5], (HEADS, HEAD_FEATURES), jnp.float32), 0.25, 1.75),
    }


def flip_strand(field_in):
    shaped = field_in.reshape(SEQUENCE_LENGTH, HEADS, HEAD_FEATURES)
    return shaped[::-1, ::-1, :].reshape(SEQUENCE_LENGTH, WIDTH)

def split_heads(field_in):
    return jnp.transpose(field_in.reshape(SEQUENCE_LENGTH, HEADS, HEAD_FEATURES), (1, 0, 2))

def join_heads(stacked):
    return jnp.transpose(stacked, (1, 0, 2)).reshape(SEQUENCE_LENGTH, WIDTH)

def listed_blocks(field_in, slot_index):
    picked = field_in.reshape(NBLOCKS, BLOCK, HEAD_FEATURES)[slot_index]
    return picked.reshape(NBLOCKS, SLOTS * BLOCK, HEAD_FEATURES).astype(jnp.float32)

def head_weights(query_head, key_head, block_mask):
    is_live = block_mask >= 0
    slot_index = jnp.where(is_live, block_mask, 0).astype(jnp.int32)
    query_block_list = query_head.reshape(NBLOCKS, BLOCK, HEAD_FEATURES).astype(jnp.float32)
    key_row_vectors = listed_blocks(key_head, slot_index)
    logit_scores = jnp.einsum('xpf,xzf->xpz', query_block_list, key_row_vectors) * HEAD_FEATURES ** (-0.5)
    columns = jnp.repeat(is_live, BLOCK, axis=1)
    logit_scores = jnp.where(columns[:, None, :], logit_scores, -1e+30)
    highest = lax.optimization_barrier(jnp.max(logit_scores, axis=-1, keepdims=True))
    powers = jnp.exp(logit_scores - highest)
    weights = powers / lax.optimization_barrier(jnp.sum(powers, axis=-1, keepdims=True))
    return (weights, slot_index, query_block_list, key_row_vectors)

def strand_forward(query_in, key_in, value_in, block_mask):

    def one_head(operands):
        query_head, key_head, value_head = operands
        weights, slot_index, query_block_list, key_row_vectors = head_weights(query_head, key_head, block_mask)
        rounded_values = lax.optimization_barrier(weights.astype(jnp.bfloat16)).astype(jnp.float32)
        value_row_vectors = listed_blocks(value_head, slot_index)
        return jnp.einsum('xes,xsg->xeg', rounded_values, value_row_vectors).reshape(SEQUENCE_LENGTH, HEAD_FEATURES)
    return join_heads(lax.map(one_head, (split_heads(query_in), split_heads(key_in), split_heads(value_in))))

def strand_backward(query_in, key_in, value_in, grad_in, block_mask):

    def one_head(operands):
        query_head, key_head, value_head, grad_head = operands
        weights, slot_index, query_block_list, key_row_vectors = head_weights(query_head, key_head, block_mask)
        rounded_values = lax.optimization_barrier(weights.astype(jnp.bfloat16)).astype(jnp.float32)
        value_row_vectors = listed_blocks(value_head, slot_index)
        gradient_block_list = grad_head.reshape(NBLOCKS, BLOCK, HEAD_FEATURES).astype(jnp.float32)
        value_contributions = jnp.einsum('xvf,xva->xfa', rounded_values, gradient_block_list)
        weight_gradient = jnp.einsum('xpf,xzf->xpz', gradient_block_list, value_row_vectors)
        centre = lax.optimization_barrier(jnp.sum(weights * weight_gradient, axis=-1, keepdims=True))
        score_gradient = lax.optimization_barrier((weights * (weight_gradient - centre)).astype(jnp.bfloat16)).astype(jnp.float32)
        query_contributions = jnp.einsum('xes,xsg->xeg', score_gradient, key_row_vectors) * HEAD_FEATURES ** (-0.5)
        key_contributions = jnp.einsum('xvf,xva->xfa', score_gradient, query_block_list) * HEAD_FEATURES ** (-0.5)
        flat_index = slot_index.reshape(NBLOCKS * SLOTS)
        key_total = jnp.zeros((NBLOCKS, BLOCK, HEAD_FEATURES), jnp.float32).at[flat_index].add(key_contributions.reshape(NBLOCKS * SLOTS, BLOCK, HEAD_FEATURES))
        value_total = jnp.zeros((NBLOCKS, BLOCK, HEAD_FEATURES), jnp.float32).at[flat_index].add(value_contributions.reshape(NBLOCKS * SLOTS, BLOCK, HEAD_FEATURES))
        return (query_contributions.reshape(SEQUENCE_LENGTH, HEAD_FEATURES), key_total.reshape(SEQUENCE_LENGTH, HEAD_FEATURES), value_total.reshape(SEQUENCE_LENGTH, HEAD_FEATURES))
    query_part, key_part, value_part = lax.map(one_head, (split_heads(query_in), split_heads(key_in), split_heads(value_in), split_heads(grad_in)))
    return (join_heads(query_part), join_heads(key_part), join_heads(value_part))

def reference(query_vecs, key_vecs, value_vecs, out_grad, block_mask, norm_gain):
    flat_gain = norm_gain.reshape(WIDTH)
    forward_part = strand_forward(query_vecs, key_vecs, value_vecs, block_mask)
    query_flip = flip_strand(query_vecs)
    key_flip = flip_strand(key_vecs)
    value_flip = flip_strand(value_vecs)
    reverse_part = flip_strand(strand_forward(query_flip, key_flip, value_flip, block_mask))
    mixed_sum = forward_part + reverse_part
    rms_root = jnp.sqrt(lax.optimization_barrier(jnp.sum(mixed_sum * mixed_sum, axis=1, keepdims=True)) / WIDTH + 1e-06)
    normed = (flat_gain * mixed_sum / rms_root).astype(jnp.bfloat16)
    grad_values = out_grad.astype(jnp.float32)
    scaled_grad = flat_gain * grad_values
    inner_sum = lax.optimization_barrier(jnp.sum(scaled_grad * mixed_sum, axis=1, keepdims=True)) / WIDTH
    mixed_grad = (scaled_grad / rms_root - mixed_sum * inner_sum / (rms_root * rms_root * rms_root)).astype(jnp.bfloat16)
    gain_grad = (lax.optimization_barrier(jnp.sum(grad_values * mixed_sum / rms_root, axis=0)) / math.sqrt(SEQUENCE_LENGTH)).reshape(HEADS, HEAD_FEATURES)
    query_one, key_one, value_one = strand_backward(query_vecs, key_vecs, value_vecs, mixed_grad, block_mask)
    query_two, key_two, value_two = strand_backward(query_flip, key_flip, value_flip, flip_strand(mixed_grad), block_mask)
    query_grad = (query_one + flip_strand(query_two)).astype(jnp.bfloat16)
    key_grad = (key_one + flip_strand(key_two)).astype(jnp.bfloat16)
    value_grad = (value_one + flip_strand(value_two)).astype(jnp.bfloat16)
    return (normed, query_grad, key_grad, value_grad, gain_grad)
```

```python
import functools
import math

import jax
import jax.numpy as jnp
from jax import lax
from jax.experimental import pallas as pl
from jax.experimental.pallas import tpu as pltpu
from jax.sharding import PartitionSpec as P

D = 128
BLOCK = 64
BAND = 2
RIM = BAND * BLOCK
PAIR = 2 * BLOCK
WINDOW = PAIR + 2 * RIM
MESH = pl.DeviceIdType.MESH
NT = (((1,), (1,)), ((), ()))
TN = (((0,), (0,)), ((), ()))
NN = (((1,), (0,)), ((), ()))


def dot(a, b, dims):
    return lax.dot_general(a, b, dims, preferred_element_type=jnp.float32)


def kernel(
    n_ctx, n_head,
    q_hbm, k_hbm, v_hbm, og_hbm, mask_ref, gain_ref,
    normed_hbm, dq_hbm, dk_hbm, dv_hbm, gg_ref,
    q, kext, vext, og, mine, theirs, bias, w1s, w2s, mixed, sq, inner, sall, invs, coefs,
    grad, gall, normed, dq, dk, dv, dko, dvo, out_halo, in_halo,
    load_sem, fsend, frecv, msend, mrecv, ssend, srecv, gsend, grecv, bsend, brecv, store_sem,
):
    pos = lax.axis_index("ctx")
    me_h = lax.axis_index("head")
    rows, features = q.shape
    heads = features // D
    pairs = rows // PAIR
    blocks_dev = rows // BLOCK
    width = features * n_head
    scale = D ** -0.5
    last = n_ctx - 1

    loads = [
        pltpu.make_async_copy(k_hbm, kext.at[pl.ds(RIM, rows)], load_sem.at[0]),
        pltpu.make_async_copy(q_hbm, q, load_sem.at[1]),
        pltpu.make_async_copy(v_hbm, vext.at[pl.ds(RIM, rows)], load_sem.at[2]),
        pltpu.make_async_copy(og_hbm, og, load_sem.at[3]),
    ]
    for copy in loads:
        copy.start()

    barrier = pltpu.get_barrier_semaphore()
    for o in range(1, n_ctx):
        pl.semaphore_signal(barrier, inc=1, device_id=(lax.rem(pos + o, n_ctx), me_h), device_id_type=MESH)
    for o in range(1, n_head):
        pl.semaphore_signal(barrier, inc=1, device_id=(pos, lax.rem(me_h + o, n_head)), device_id_type=MESH)
    mine[...] = jnp.zeros_like(mine)
    mine[0:blocks_dev, 0:mask_ref.shape[1]] = mask_ref[...]
    sall[me_h] = jnp.zeros(sall.shape[1:], jnp.float32)
    sq[...] = jnp.zeros_like(sq)
    inner[...] = jnp.zeros_like(inner)

    @pl.when(pos == 0)
    def _():
        kext[0:RIM, :] = jnp.zeros((RIM, features), kext.dtype)
        vext[0:RIM, :] = jnp.zeros((RIM, features), vext.dtype)

    @pl.when(pos == last)
    def _():
        kext[rows + RIM :, :] = jnp.zeros((RIM, features), kext.dtype)
        vext[rows + RIM :, :] = jnp.zeros((RIM, features), vext.dtype)

    pl.semaphore_wait(barrier, n_ctx - 1 + n_head - 1)

    def cols(h):
        return pl.ds(pl.multiple_of(h * D, D), D)

    right = jnp.minimum(pos + 1, last)
    left = jnp.maximum(pos - 1, 0)

    def halo(way, kv, h):
        src = (k_hbm, v_hbm)[kv]
        dst = (kext, vext)[kv]
        from_row, to_row = ((rows - RIM, 0), (0, rows + RIM))[way]
        return pltpu.make_async_remote_copy(
            src_ref=src.at[pl.ds(from_row, RIM), cols(h)],
            dst_ref=dst.at[pl.ds(to_row, RIM), cols(h)],
            send_sem=fsend.at[way, kv, h],
            recv_sem=frecv.at[way, kv, h],
            device_id=((right, left)[way], me_h),
            device_id_type=MESH,
        )

    mirror = pltpu.make_async_remote_copy(
        src_ref=mine, dst_ref=theirs, send_sem=msend, recv_sem=mrecv,
        device_id=(last - pos, me_h), device_id_type=MESH,
    )
    mirror.start()

    def send_halos(h, carry):
        for kv in range(2):
            @pl.when(pos < last)
            def _():
                halo(0, kv, h).start()

            @pl.when(pos > 0)
            def _():
                halo(1, kv, h).start()
        return carry

    lax.fori_loop(0, heads, send_halos, 0)
    mirror.wait_recv()

    all_blocks = blocks_dev * n_ctx
    row_block = lax.broadcasted_iota(jnp.int32, (WINDOW, PAIR), 0) // BLOCK
    second = lax.broadcasted_iota(jnp.int32, (8, PAIR), 1) >= BLOCK
    for strand in range(2):
        table = (mine, theirs)[strand]
        for p in range(pairs):
            first = pos * blocks_dev - BAND + 2 * p
            live = None
            for n in range(mask_ref.shape[1]):
                lists = []
                for b in (2 * p, 2 * p + 1):
                    r = b if strand == 0 else blocks_dev - 1 - b
                    lists.append(jnp.broadcast_to(table[r : r + 1, n : n + 1], (8, PAIR)))
                entry = jnp.where(second, lists[1], lists[0])
                if strand == 1:
                    target = all_blocks - 1 - entry
                else:
                    target = entry
                target = jnp.where(entry >= 0, target - first, -1)[0:1]
                hit = row_block == target
                live = hit if live is None else live | hit
            bias[strand, p] = jnp.where(live, 0.0, -1e30)

    for copy in loads:
        copy.wait()

    def forward(h, carry):
        c = cols(h)
        for kv in range(2):
            @pl.when(pos > 0)
            def _():
                halo(0, kv, h).wait_recv()

            @pl.when(pos < last)
            def _():
                halo(1, kv, h).wait_recv()
        gain = gain_ref[pl.ds(h, 1), :]
        for p in range(pairs):
            r = pl.ds(p * PAIR, PAIR)
            w = pl.ds(p * PAIR, WINDOW)
            scores = dot(kext[w, c], q[r, c], NT) * scale
            total = None
            for strand, kept in ((0, w1s), (1, w2s)):
                s = scores + bias[strand, p]
                e = jnp.exp(s - jnp.max(s, axis=0, keepdims=True))
                e = e * (1.0 / jnp.sum(e, axis=0, keepdims=True))
                kept[h, p] = e
                total = e if total is None else total + e
            m = dot(total.astype(jnp.bfloat16), vext[w, c], TN)
            mixed[r, c] = m
            sq[r, :] += m * m
            inner[r, :] += gain * og[r, c].astype(jnp.float32) * m
        return carry

    lax.fori_loop(0, heads, forward, 0)

    for p in range(pairs):
        r = slice(p * PAIR, (p + 1) * PAIR)
        sall[me_h, p : p + 1, :] = jnp.sum(sq[r, :].T, axis=0, keepdims=True)
        sall[me_h, pairs + p : pairs + p + 1, :] = jnp.sum(inner[r, :].T, axis=0, keepdims=True)

    def stat(slot, o, to):
        return pltpu.make_async_remote_copy(
            src_ref=sall.at[slot], dst_ref=sall.at[slot],
            send_sem=ssend.at[o], recv_sem=srecv.at[slot],
            device_id=(pos, to), device_id_type=MESH,
        )

    for o in range(1, n_head):
        stat(me_h, o, lax.rem(me_h + o, n_head)).start()
    for o in range(1, n_head):
        stat(lax.rem(me_h + o, n_head), o, me_h).wait_recv()
    tot = sall[0]
    for s in range(1, n_head):
        tot = tot + sall[s]
    inv = 1.0 / jnp.sqrt(tot[0:pairs] / width + 1e-06)
    coef = tot[pairs : 2 * pairs] / width * (inv * inv * inv)
    for p in range(pairs):
        r = slice(p * PAIR, (p + 1) * PAIR)
        invs[r, :] = jnp.broadcast_to(inv[p : p + 1], (PAIR, D)).T
        coefs[r, :] = jnp.broadcast_to(coef[p : p + 1], (PAIR, D)).T

    def normalise(h, carry):
        c = cols(h)
        gain = gain_ref[pl.ds(h, 1), :]
        m = mixed[:, c]
        g = og[:, c].astype(jnp.float32)
        iv = invs[...]
        mi = m * iv
        normed[:, c] = (gain * mi).astype(jnp.bfloat16)
        grad[:, c] = (gain * g * iv - m * coefs[...]).astype(jnp.bfloat16)
        gall[pos, pl.ds(h, 1), :] = jnp.sum(g * mi, axis=0, keepdims=True)
        return carry

    lax.fori_loop(0, heads, normalise, 0)

    def share(slot, o, to):
        return pltpu.make_async_remote_copy(
            src_ref=gall.at[slot], dst_ref=gall.at[slot],
            send_sem=gsend.at[o], recv_sem=grecv.at[slot],
            device_id=(to, me_h), device_id_type=MESH,
        )

    for o in range(1, n_ctx):
        share(pos, o, lax.rem(pos + o, n_ctx)).start()
    out_copies = [pltpu.make_async_copy(normed, normed_hbm, store_sem.at[0])]
    out_copies[0].start()

    def back(way, kv, h):
        return pltpu.make_async_remote_copy(
            src_ref=out_halo.at[way, kv, :, cols(h)],
            dst_ref=in_halo.at[way, kv, :, cols(h)],
            send_sem=bsend.at[way, kv, h],
            recv_sem=brecv.at[way, kv, h],
            device_id=((right, left)[way], me_h),
            device_id_type=MESH,
        )

    def backward(h, carry):
        c = cols(h)
        parts = []
        for p in range(pairs):
            r = pl.ds(p * PAIR, PAIR)
            w = pl.ds(p * PAIR, WINDOW)
            g = grad[r, c]
            w1, w2 = w1s[h, p], w2s[h, p]
            wg = dot(vext[w, c], g, NT)
            c1 = jnp.sum(w1 * wg, axis=0, keepdims=True)
            c2 = jnp.sum(w2 * wg, axis=0, keepdims=True)
            ds = ((w1 * (wg - c1) + w2 * (wg - c2)) * scale).astype(jnp.bfloat16)
            dvw = dot((w1 + w2).astype(jnp.bfloat16), g, NN)
            dkw = dot(ds, q[r, c], NN)
            dq[r, c] = dot(ds, kext[w, c], TN).astype(jnp.bfloat16)
            parts.append((dkw, dvw))
        for kv, own in ((0, dk), (1, dv)):
            out_halo[1, kv, :, c] = parts[0][kv][0:RIM].astype(jnp.bfloat16)
            out_halo[0, kv, :, c] = parts[-1][kv][WINDOW - RIM :].astype(jnp.bfloat16)
            for p in range(pairs):
                mid = parts[p][kv][RIM : RIM + PAIR]
                if p > 0:
                    mid = mid + parts[p - 1][kv][RIM + PAIR :]
                if p < pairs - 1:
                    mid = mid + parts[p + 1][kv][0:RIM]
                own[pl.ds(p * PAIR, PAIR), c] = mid

            @pl.when(pos < last)
            def _():
                back(0, kv, h).start()

            @pl.when(pos > 0)
            def _():
                back(1, kv, h).start()
        return carry

    lax.fori_loop(0, heads, backward, 0)
    dq_copy = pltpu.make_async_copy(dq, dq_hbm, store_sem.at[1])
    dq_copy.start()
    out_copies.append(dq_copy)

    for o in range(1, n_ctx):
        share(lax.rem(pos + o, n_ctx), o, pos).wait_recv()
    total = gall[0]
    for s in range(1, n_ctx):
        total = total + gall[s]
    gg_ref[...] = total / math.sqrt(rows * n_ctx)

    @pl.when(pos == 0)
    def _():
        in_halo[0] = jnp.zeros(in_halo.shape[1:], in_halo.dtype)

    @pl.when(pos == last)
    def _():
        in_halo[1] = jnp.zeros(in_halo.shape[1:], in_halo.dtype)

    def settle(h, carry):
        c = cols(h)
        for kv, own, out in ((0, dk, dko), (1, dv, dvo)):
            @pl.when(pos > 0)
            def _():
                back(0, kv, h).wait_recv()

            @pl.when(pos < last)
            def _():
                back(1, kv, h).wait_recv()
            out[0:RIM, c] = (own[0:RIM, c] + in_halo[0, kv, :, c].astype(jnp.float32)).astype(jnp.bfloat16)
            out[rows - RIM : rows, c] = (
                own[rows - RIM : rows, c] + in_halo[1, kv, :, c].astype(jnp.float32)
            ).astype(jnp.bfloat16)
        return carry

    lax.fori_loop(0, heads, settle, 0)
    for i, (src, dst) in enumerate(((dko, dk_hbm), (dvo, dv_hbm))):
        copy = pltpu.make_async_copy(src, dst, store_sem.at[2 + i])
        copy.start()
        out_copies.append(copy)

    mirror.wait_send()
    for o in range(1, n_head):
        stat(me_h, o, lax.rem(me_h + o, n_head)).wait_send()
    for o in range(1, n_ctx):
        share(pos, o, lax.rem(pos + o, n_ctx)).wait_send()

    def drain(h, carry):
        for kv in range(2):
            @pl.when(pos < last)
            def _():
                halo(0, kv, h).wait_send()
                back(0, kv, h).wait_send()

            @pl.when(pos > 0)
            def _():
                halo(1, kv, h).wait_send()
                back(1, kv, h).wait_send()
        return carry

    lax.fori_loop(0, heads, drain, 0)
    for copy in out_copies:
        copy.wait()


def body(query_vecs, key_vecs, value_vecs, out_grad, block_mask, norm_gain):
    n_ctx = lax.axis_size("ctx")
    n_head = lax.axis_size("head")
    rows, features = query_vecs.shape
    heads = features // D
    pairs = rows // PAIR
    ext = rows + 2 * RIM
    bf, f32 = jnp.bfloat16, jnp.float32
    dma = pltpu.SemaphoreType.DMA
    hbm = pl.BlockSpec(memory_space=pl.ANY)
    vmem = pl.BlockSpec(memory_space=pltpu.VMEM)
    big = jax.ShapeDtypeStruct((rows, features), bf)
    return pl.pallas_call(
        functools.partial(kernel, n_ctx, n_head),
        out_shape=(big, big, big, big, jax.ShapeDtypeStruct((heads, D), f32)),
        in_specs=[hbm, hbm, hbm, hbm, vmem, vmem],
        out_specs=(hbm, hbm, hbm, hbm, vmem),
        scratch_shapes=[
            pltpu.VMEM((rows, features), bf),
            pltpu.VMEM((ext, features), bf),
            pltpu.VMEM((ext, features), bf),
            pltpu.VMEM((rows, features), bf),
            pltpu.VMEM((8, 128), jnp.int32),
            pltpu.VMEM((8, 128), jnp.int32),
            pltpu.VMEM((2, pairs, WINDOW, PAIR), f32),
            pltpu.VMEM((heads, pairs, WINDOW, PAIR), f32),
            pltpu.VMEM((heads, pairs, WINDOW, PAIR), f32),
            pltpu.VMEM((rows, features), f32),
            pltpu.VMEM((rows, D), f32),
            pltpu.VMEM((rows, D), f32),
            pltpu.VMEM((n_head, 8, PAIR), f32),
            pltpu.VMEM((rows, D), f32),
            pltpu.VMEM((rows, D), f32),
            pltpu.VMEM((rows, features), bf),
            pltpu.VMEM((n_ctx, heads, D), f32),
            pltpu.VMEM((rows, features), bf),
            pltpu.VMEM((rows, features), bf),
            pltpu.VMEM((rows, features), f32),
            pltpu.VMEM((rows, features), f32),
            pltpu.VMEM((rows, features), bf),
            pltpu.VMEM((rows, features), bf),
            pltpu.VMEM((2, 2, RIM, features), bf),
            pltpu.VMEM((2, 2, RIM, features), bf),
            dma((4,)),
            dma((2, 2, heads)),
            dma((2, 2, heads)),
            dma,
            dma,
            dma((n_head,)),
            dma((n_head,)),
            dma((n_ctx,)),
            dma((n_ctx,)),
            dma((2, 2, heads)),
            dma((2, 2, heads)),
            dma((4,)),
        ],
        compiler_params=pltpu.CompilerParams(
            collective_id=0, has_side_effects=True, vmem_limit_bytes=48 * 1024 * 1024
        ),
        name="strand_attention",
    )(query_vecs, key_vecs, value_vecs, out_grad, block_mask, norm_gain)


def solution(mesh):
    tokens = P("ctx", "head")
    return jax.shard_map(
        body,
        mesh=mesh,
        in_specs=(tokens, tokens, tokens, tokens, P("ctx", None), P("head", None)),
        out_specs=(tokens, tokens, tokens, tokens, P("head", None)),
        check_vma=False,
    )
```

```python
import functools
import math

import jax
import jax.numpy as jnp
from jax import lax
from jax.experimental import pallas as pl
from jax.experimental.pallas import tpu as pltpu
from jax.sharding import PartitionSpec as P

D = 128
BLOCK = 64
BAND = 2
RIM = BAND * BLOCK
PAIR = 2 * BLOCK
WINDOW = PAIR + 2 * RIM
VMEM = 64 * 1024 * 1024
MESH = pl.DeviceIdType.MESH
NT = (((1,), (1,)), ((), ()))
TN = (((0,), (0,)), ((), ()))
NN = (((1,), (0,)), ((), ()))


def dot(a, b, dims):
    return lax.dot_general(a, b, dims, preferred_element_type=jnp.float32)


def kernel(
    n_ctx, n_head,
    q_hbm, k_hbm, v_hbm, og_hbm, mask_hbm, gain_hbm,
    normed_hbm, dq_hbm, dk_hbm, dv_hbm, gg_ref,
    mask_ref, gain_ref, q, kext, vext, og, mine, theirs, bias, w1s, w2s, mixed, sq, inner, sall, invs, coefs,
    grad, gall, normed, dq, dk, dv, dko, dvo, out_halo, in_halo,
    load_sem, fsend, frecv, msend, mrecv, ssend, srecv, gsend, grecv, bsend, brecv, store_sem,
):
    pos = lax.axis_index("ctx")
    me_h = lax.axis_index("head")
    rows, features = q.shape
    heads = features // D
    pairs = rows // PAIR
    blocks_dev = rows // BLOCK
    width = features * n_head
    scale = D ** -0.5
    last = n_ctx - 1

    small = [
        pltpu.make_async_copy(mask_hbm, mask_ref, load_sem.at[4]),
        pltpu.make_async_copy(gain_hbm, gain_ref, load_sem.at[5]),
    ]
    loads = [
        pltpu.make_async_copy(k_hbm, kext.at[pl.ds(RIM, rows)], load_sem.at[0]),
        pltpu.make_async_copy(q_hbm, q, load_sem.at[1]),
        pltpu.make_async_copy(v_hbm, vext.at[pl.ds(RIM, rows)], load_sem.at[2]),
        pltpu.make_async_copy(og_hbm, og, load_sem.at[3]),
    ]
    for copy in small + loads:
        copy.start()

    barrier = pltpu.get_barrier_semaphore()
    for o in range(1, n_ctx):
        pl.semaphore_signal(barrier, inc=1, device_id=(lax.rem(pos + o, n_ctx), me_h), device_id_type=MESH)
    for o in range(1, n_head):
        pl.semaphore_signal(barrier, inc=1, device_id=(pos, lax.rem(me_h + o, n_head)), device_id_type=MESH)
    mine[...] = jnp.zeros_like(mine)
    for copy in small:
        copy.wait()
    mine[0:blocks_dev, 0:mask_ref.shape[1]] = mask_ref[...]
    sall[me_h] = jnp.zeros(sall.shape[1:], jnp.float32)
    sq[...] = jnp.zeros_like(sq)
    inner[...] = jnp.zeros_like(inner)

    @pl.when(pos == 0)
    def _():
        kext[0:RIM, :] = jnp.zeros((RIM, features), kext.dtype)
        vext[0:RIM, :] = jnp.zeros((RIM, features), vext.dtype)

    @pl.when(pos == last)
    def _():
        kext[rows + RIM :, :] = jnp.zeros((RIM, features), kext.dtype)
        vext[rows + RIM :, :] = jnp.zeros((RIM, features), vext.dtype)

    pl.semaphore_wait(barrier, n_ctx - 1 + n_head - 1)

    def cols(h):
        return pl.ds(pl.multiple_of(h * D, D), D)

    right = jnp.minimum(pos + 1, last)
    left = jnp.maximum(pos - 1, 0)

    def halo(way, kv, h):
        src = (k_hbm, v_hbm)[kv]
        dst = (kext, vext)[kv]
        from_row, to_row = ((rows - RIM, 0), (0, rows + RIM))[way]
        return pltpu.make_async_remote_copy(
            src_ref=src.at[pl.ds(from_row, RIM), cols(h)],
            dst_ref=dst.at[pl.ds(to_row, RIM), cols(h)],
            send_sem=fsend.at[way, kv, h],
            recv_sem=frecv.at[way, kv, h],
            device_id=((right, left)[way], me_h),
            device_id_type=MESH,
        )

    mirror = pltpu.make_async_remote_copy(
        src_ref=mine, dst_ref=theirs, send_sem=msend, recv_sem=mrecv,
        device_id=(last - pos, me_h), device_id_type=MESH,
    )
    mirror.start()

    def send_halos(h, carry):
        for kv in range(2):
            @pl.when(pos < last)
            def _():
                halo(0, kv, h).start()

            @pl.when(pos > 0)
            def _():
                halo(1, kv, h).start()
        return carry

    lax.fori_loop(0, heads, send_halos, 0)
    mirror.wait_recv()

    all_blocks = blocks_dev * n_ctx
    row_block = lax.broadcasted_iota(jnp.int32, (WINDOW, PAIR), 0) // BLOCK
    second = lax.broadcasted_iota(jnp.int32, (8, PAIR), 1) >= BLOCK
    for strand in range(2):
        table = (mine, theirs)[strand]
        for p in range(pairs):
            first = pos * blocks_dev - BAND + 2 * p
            live = None
            for n in range(mask_ref.shape[1]):
                lists = []
                for b in (2 * p, 2 * p + 1):
                    r = b if strand == 0 else blocks_dev - 1 - b
                    lists.append(jnp.broadcast_to(table[r : r + 1, n : n + 1], (8, PAIR)))
                entry = jnp.where(second, lists[1], lists[0])
                if strand == 1:
                    target = all_blocks - 1 - entry
                else:
                    target = entry
                target = jnp.where(entry >= 0, target - first, -1)[0:1]
                hit = row_block == target
                live = hit if live is None else live | hit
            bias[strand, p] = jnp.where(live, 0.0, -1e30)

    for copy in loads:
        copy.wait()

    def forward(h, carry):
        c = cols(h)
        for kv in range(2):
            @pl.when(pos > 0)
            def _():
                halo(0, kv, h).wait_recv()

            @pl.when(pos < last)
            def _():
                halo(1, kv, h).wait_recv()
        gain = gain_ref[pl.ds(h, 1), :]
        for p in range(pairs):
            r = pl.ds(p * PAIR, PAIR)
            w = pl.ds(p * PAIR, WINDOW)
            scores = dot(kext[w, c], q[r, c], NT) * scale
            total = None
            for strand, kept in ((0, w1s), (1, w2s)):
                s = scores + bias[strand, p]
                e = jnp.exp(s - jnp.max(s, axis=0, keepdims=True))
                e = e * (1.0 / jnp.sum(e, axis=0, keepdims=True))
                kept[h, p] = e
                total = e if total is None else total + e
            m = dot(total.astype(jnp.bfloat16), vext[w, c], TN)
            mixed[r, c] = m
            sq[r, :] += m * m
            inner[r, :] += gain * og[r, c].astype(jnp.float32) * m
        return carry

    lax.fori_loop(0, heads, forward, 0)

    for p in range(pairs):
        r = slice(p * PAIR, (p + 1) * PAIR)
        sall[me_h, p : p + 1, :] = jnp.sum(sq[r, :].T, axis=0, keepdims=True)
        sall[me_h, pairs + p : pairs + p + 1, :] = jnp.sum(inner[r, :].T, axis=0, keepdims=True)

    def stat(slot, o, to):
        return pltpu.make_async_remote_copy(
            src_ref=sall.at[slot], dst_ref=sall.at[slot],
            send_sem=ssend.at[o], recv_sem=srecv.at[slot],
            device_id=(pos, to), device_id_type=MESH,
        )

    for o in range(1, n_head):
        stat(me_h, o, lax.rem(me_h + o, n_head)).start()
    for o in range(1, n_head):
        stat(lax.rem(me_h + o, n_head), o, me_h).wait_recv()
    tot = sall[0]
    for s in range(1, n_head):
        tot = tot + sall[s]
    inv = 1.0 / jnp.sqrt(tot[0:pairs] / width + 1e-06)
    coef = tot[pairs : 2 * pairs] / width * (inv * inv * inv)
    for p in range(pairs):
        r = slice(p * PAIR, (p + 1) * PAIR)
        invs[r, :] = jnp.broadcast_to(inv[p : p + 1], (PAIR, D)).T
        coefs[r, :] = jnp.broadcast_to(coef[p : p + 1], (PAIR, D)).T

    def normalise(h, carry):
        c = cols(h)
        gain = gain_ref[pl.ds(h, 1), :]
        m = mixed[:, c]
        g = og[:, c].astype(jnp.float32)
        iv = invs[...]
        mi = m * iv
        normed[:, c] = (gain * mi).astype(jnp.bfloat16)
        grad[:, c] = (gain * g * iv - m * coefs[...]).astype(jnp.bfloat16)
        gall[pos, pl.ds(h, 1), :] = jnp.sum(g * mi, axis=0, keepdims=True)
        return carry

    lax.fori_loop(0, heads, normalise, 0)

    def share(slot, o, to):
        return pltpu.make_async_remote_copy(
            src_ref=gall.at[slot], dst_ref=gall.at[slot],
            send_sem=gsend.at[o], recv_sem=grecv.at[slot],
            device_id=(to, me_h), device_id_type=MESH,
        )

    for o in range(1, n_ctx):
        share(pos, o, lax.rem(pos + o, n_ctx)).start()
    out_copies = [pltpu.make_async_copy(normed, normed_hbm, store_sem.at[0])]
    out_copies[0].start()

    def back(way, kv, h):
        return pltpu.make_async_remote_copy(
            src_ref=out_halo.at[way, kv, :, cols(h)],
            dst_ref=in_halo.at[way, kv, :, cols(h)],
            send_sem=bsend.at[way, kv, h],
            recv_sem=brecv.at[way, kv, h],
            device_id=((right, left)[way], me_h),
            device_id_type=MESH,
        )

    def backward(h, carry):
        c = cols(h)
        parts = []
        for p in range(pairs):
            r = pl.ds(p * PAIR, PAIR)
            w = pl.ds(p * PAIR, WINDOW)
            g = grad[r, c]
            w1, w2 = w1s[h, p], w2s[h, p]
            wg = dot(vext[w, c], g, NT)
            c1 = jnp.sum(w1 * wg, axis=0, keepdims=True)
            c2 = jnp.sum(w2 * wg, axis=0, keepdims=True)
            ds = ((w1 * (wg - c1) + w2 * (wg - c2)) * scale).astype(jnp.bfloat16)
            dvw = dot((w1 + w2).astype(jnp.bfloat16), g, NN)
            dkw = dot(ds, q[r, c], NN)
            dq[r, c] = dot(ds, kext[w, c], TN).astype(jnp.bfloat16)
            parts.append((dkw, dvw))
        for kv, own in ((0, dk), (1, dv)):
            out_halo[1, kv, :, c] = parts[0][kv][0:RIM].astype(jnp.bfloat16)
            out_halo[0, kv, :, c] = parts[-1][kv][WINDOW - RIM :].astype(jnp.bfloat16)
            for p in range(pairs):
                mid = parts[p][kv][RIM : RIM + PAIR]
                if p > 0:
                    mid = mid + parts[p - 1][kv][RIM + PAIR :]
                if p < pairs - 1:
                    mid = mid + parts[p + 1][kv][0:RIM]
                own[pl.ds(p * PAIR, PAIR), c] = mid

            @pl.when(pos < last)
            def _():
                back(0, kv, h).start()

            @pl.when(pos > 0)
            def _():
                back(1, kv, h).start()
        return carry

    lax.fori_loop(0, heads, backward, 0)
    dq_copy = pltpu.make_async_copy(dq, dq_hbm, store_sem.at[1])
    dq_copy.start()
    out_copies.append(dq_copy)

    for o in range(1, n_ctx):
        share(lax.rem(pos + o, n_ctx), o, pos).wait_recv()
    total = gall[0]
    for s in range(1, n_ctx):
        total = total + gall[s]
    gg_ref[...] = total / math.sqrt(rows * n_ctx)

    @pl.when(pos == 0)
    def _():
        in_halo[0] = jnp.zeros(in_halo.shape[1:], in_halo.dtype)

    @pl.when(pos == last)
    def _():
        in_halo[1] = jnp.zeros(in_halo.shape[1:], in_halo.dtype)

    def settle(h, carry):
        c = cols(h)
        for kv, own, out in ((0, dk, dko), (1, dv, dvo)):
            @pl.when(pos > 0)
            def _():
                back(0, kv, h).wait_recv()

            @pl.when(pos < last)
            def _():
                back(1, kv, h).wait_recv()
            out[0:RIM, c] = (own[0:RIM, c] + in_halo[0, kv, :, c].astype(jnp.float32)).astype(jnp.bfloat16)
            out[rows - RIM : rows, c] = (
                own[rows - RIM : rows, c] + in_halo[1, kv, :, c].astype(jnp.float32)
            ).astype(jnp.bfloat16)
        return carry

    lax.fori_loop(0, heads, settle, 0)
    for i, (src, dst) in enumerate(((dko, dk_hbm), (dvo, dv_hbm))):
        copy = pltpu.make_async_copy(src, dst, store_sem.at[2 + i])
        copy.start()
        out_copies.append(copy)

    mirror.wait_send()
    for o in range(1, n_head):
        stat(me_h, o, lax.rem(me_h + o, n_head)).wait_send()
    for o in range(1, n_ctx):
        share(pos, o, lax.rem(pos + o, n_ctx)).wait_send()

    def drain(h, carry):
        for kv in range(2):
            @pl.when(pos < last)
            def _():
                halo(0, kv, h).wait_send()
                back(0, kv, h).wait_send()

            @pl.when(pos > 0)
            def _():
                halo(1, kv, h).wait_send()
                back(1, kv, h).wait_send()
        return carry

    lax.fori_loop(0, heads, drain, 0)
    for copy in out_copies:
        copy.wait()


def store_kernel(*refs):
    count = len(refs) // 2
    sems = refs[-1]
    copies = [pltpu.make_async_copy(refs[i], refs[count + i], sems.at[i]) for i in range(count)]
    for copy in copies:
        copy.start()
    for copy in copies:
        copy.wait()


def body(query_vecs, key_vecs, value_vecs, out_grad, block_mask, norm_gain):
    n_ctx = lax.axis_size("ctx")
    n_head = lax.axis_size("head")
    rows, features = query_vecs.shape
    heads = features // D
    pairs = rows // PAIR
    ext = rows + 2 * RIM
    bf, f32 = jnp.bfloat16, jnp.float32
    dma = pltpu.SemaphoreType.DMA
    hbm = pl.BlockSpec(memory_space=pl.ANY)
    vmem = pl.BlockSpec(memory_space=pltpu.VMEM)
    fixed = pl.BlockSpec(memory_space=pltpu.HBM)
    big = jax.ShapeDtypeStruct((rows, features), bf)
    results = pl.pallas_call(
        functools.partial(kernel, n_ctx, n_head),
        out_shape=(big, big, big, big, jax.ShapeDtypeStruct((heads, D), f32)),
        in_specs=[fixed] * 6,
        out_specs=(hbm, hbm, hbm, hbm, vmem),
        scratch_shapes=[
            pltpu.VMEM(block_mask.shape, jnp.int32),
            pltpu.VMEM(norm_gain.shape, f32),
            pltpu.VMEM((rows, features), bf),
            pltpu.VMEM((ext, features), bf),
            pltpu.VMEM((ext, features), bf),
            pltpu.VMEM((rows, features), bf),
            pltpu.VMEM((8, 128), jnp.int32),
            pltpu.VMEM((8, 128), jnp.int32),
            pltpu.VMEM((2, pairs, WINDOW, PAIR), f32),
            pltpu.VMEM((heads, pairs, WINDOW, PAIR), f32),
            pltpu.VMEM((heads, pairs, WINDOW, PAIR), f32),
            pltpu.VMEM((rows, features), f32),
            pltpu.VMEM((rows, D), f32),
            pltpu.VMEM((rows, D), f32),
            pltpu.VMEM((n_head, 8, PAIR), f32),
            pltpu.VMEM((rows, D), f32),
            pltpu.VMEM((rows, D), f32),
            pltpu.VMEM((rows, features), bf),
            pltpu.VMEM((n_ctx, heads, D), f32),
            pltpu.VMEM((rows, features), bf),
            pltpu.VMEM((rows, features), bf),
            pltpu.VMEM((rows, features), f32),
            pltpu.VMEM((rows, features), f32),
            pltpu.VMEM((rows, features), bf),
            pltpu.VMEM((rows, features), bf),
            pltpu.VMEM((2, 2, RIM, features), bf),
            pltpu.VMEM((2, 2, RIM, features), bf),
            dma((6,)),
            dma((2, 2, heads)),
            dma((2, 2, heads)),
            dma,
            dma,
            dma((n_head,)),
            dma((n_head,)),
            dma((n_ctx,)),
            dma((n_ctx,)),
            dma((2, 2, heads)),
            dma((2, 2, heads)),
            dma((4,)),
        ],
        compiler_params=pltpu.CompilerParams(
            collective_id=0, has_side_effects=True, vmem_limit_bytes=VMEM
        ),
        name="strand_attention",
    )(query_vecs, key_vecs, value_vecs, out_grad, block_mask, norm_gain)
    return pl.pallas_call(
        store_kernel,
        out_shape=tuple(jax.ShapeDtypeStruct(x.shape, x.dtype) for x in results),
        in_specs=[hbm] * 5,
        out_specs=(fixed,) * 5,
        scratch_shapes=[dma((5,))],
        compiler_params=pltpu.CompilerParams(vmem_limit_bytes=VMEM),
        name="store_results",
    )(*results)


def solution(mesh):
    tokens = P("ctx", "head")
    return jax.shard_map(
        body,
        mesh=mesh,
        in_specs=(tokens, tokens, tokens, tokens, P("ctx", None), P("head", None)),
        out_specs=(tokens, tokens, tokens, tokens, P("head", None)),
        check_vma=False,
    )
```

```python
import functools
import math

import jax
import jax.numpy as jnp
from jax import lax
from jax.experimental import pallas as pl
from jax.experimental.pallas import tpu as pltpu
from jax.sharding import PartitionSpec as P

D = 128
BLOCK = 64
BAND = 2
RIM = BAND * BLOCK
PAIR = 2 * BLOCK
WINDOW = PAIR + 2 * RIM
VMEM = 64 * 1024 * 1024
GROUP = 2
MESH = pl.DeviceIdType.MESH
NT = (((1,), (1,)), ((), ()))
TN = (((0,), (0,)), ((), ()))
NN = (((1,), (0,)), ((), ()))


def dot(a, b, dims):
    return lax.dot_general(a, b, dims, preferred_element_type=jnp.float32)


def kernel(
    n_ctx, n_head,
    q_hbm, k_hbm, v_hbm, og_hbm, mask_hbm, gain_hbm,
    normed_hbm, dq_hbm, dk_hbm, dv_hbm, gg_ref,
    mask_ref, gain_ref, q, kext, vext, og, mine, theirs, bias, w1s, w2s, mixed, sq, inner, sall, invs, coefs,
    grad, gall, normed, dq, dk, dv, dko, dvo, out_halo, in_halo,
    load_sem, fsend, frecv, msend, mrecv, ssend, srecv, gsend, grecv, bsend, brecv, store_sem,
):
    pos = lax.axis_index("ctx")
    me_h = lax.axis_index("head")
    rows, features = q.shape
    heads = features // D
    pairs = rows // PAIR
    blocks_dev = rows // BLOCK
    width = features * n_head
    scale = D ** -0.5
    last = n_ctx - 1

    small = [
        pltpu.make_async_copy(mask_hbm, mask_ref, load_sem.at[4]),
        pltpu.make_async_copy(gain_hbm, gain_ref, load_sem.at[5]),
    ]
    loads = [
        pltpu.make_async_copy(k_hbm, kext.at[pl.ds(RIM, rows)], load_sem.at[0]),
        pltpu.make_async_copy(q_hbm, q, load_sem.at[1]),
        pltpu.make_async_copy(v_hbm, vext.at[pl.ds(RIM, rows)], load_sem.at[2]),
        pltpu.make_async_copy(og_hbm, og, load_sem.at[3]),
    ]
    for copy in small + loads:
        copy.start()

    barrier = pltpu.get_barrier_semaphore()
    for o in range(1, n_ctx):
        pl.semaphore_signal(barrier, inc=1, device_id=(lax.rem(pos + o, n_ctx), me_h), device_id_type=MESH)
    for o in range(1, n_head):
        pl.semaphore_signal(barrier, inc=1, device_id=(pos, lax.rem(me_h + o, n_head)), device_id_type=MESH)
    mine[...] = jnp.zeros_like(mine)
    for copy in small:
        copy.wait()
    mine[0:blocks_dev, 0:mask_ref.shape[1]] = mask_ref[...]
    sall[me_h] = jnp.zeros(sall.shape[1:], jnp.float32)
    sq[...] = jnp.zeros_like(sq)
    inner[...] = jnp.zeros_like(inner)

    @pl.when(pos == 0)
    def _():
        kext[0:RIM, :] = jnp.zeros((RIM, features), kext.dtype)
        vext[0:RIM, :] = jnp.zeros((RIM, features), vext.dtype)

    @pl.when(pos == last)
    def _():
        kext[rows + RIM :, :] = jnp.zeros((RIM, features), kext.dtype)
        vext[rows + RIM :, :] = jnp.zeros((RIM, features), vext.dtype)

    pl.semaphore_wait(barrier, n_ctx - 1 + n_head - 1)

    def cols(h):
        return pl.ds(pl.multiple_of(h * D, D), D)

    right = jnp.minimum(pos + 1, last)
    left = jnp.maximum(pos - 1, 0)

    def halo(way, kv, h):
        src = (k_hbm, v_hbm)[kv]
        dst = (kext, vext)[kv]
        from_row, to_row = ((rows - RIM, 0), (0, rows + RIM))[way]
        return pltpu.make_async_remote_copy(
            src_ref=src.at[pl.ds(from_row, RIM), cols(h)],
            dst_ref=dst.at[pl.ds(to_row, RIM), cols(h)],
            send_sem=fsend.at[way, kv, h],
            recv_sem=frecv.at[way, kv, h],
            device_id=((right, left)[way], me_h),
            device_id_type=MESH,
        )

    mirror = pltpu.make_async_remote_copy(
        src_ref=mine, dst_ref=theirs, send_sem=msend, recv_sem=mrecv,
        device_id=(last - pos, me_h), device_id_type=MESH,
    )
    mirror.start()

    def send_halos(h, carry):
        for kv in range(2):
            @pl.when(pos < last)
            def _():
                halo(0, kv, h).start()

            @pl.when(pos > 0)
            def _():
                halo(1, kv, h).start()
        return carry

    lax.fori_loop(0, heads, send_halos, 0)
    mirror.wait_recv()

    all_blocks = blocks_dev * n_ctx
    row_block = lax.broadcasted_iota(jnp.int32, (WINDOW, PAIR), 0) // BLOCK
    second = lax.broadcasted_iota(jnp.int32, (8, PAIR), 1) >= BLOCK
    for strand in range(2):
        table = (mine, theirs)[strand]
        for p in range(pairs):
            first = pos * blocks_dev - BAND + 2 * p
            live = None
            for n in range(mask_ref.shape[1]):
                lists = []
                for b in (2 * p, 2 * p + 1):
                    r = b if strand == 0 else blocks_dev - 1 - b
                    lists.append(jnp.broadcast_to(table[r : r + 1, n : n + 1], (8, PAIR)))
                entry = jnp.where(second, lists[1], lists[0])
                if strand == 1:
                    target = all_blocks - 1 - entry
                else:
                    target = entry
                target = jnp.where(entry >= 0, target - first, -1)[0:1]
                hit = row_block == target
                live = hit if live is None else live | hit
            bias[strand, p] = jnp.where(live, 0.0, -1e30)

    for copy in loads:
        copy.wait()

    def forward(step, carry):
        group = [step * GROUP + i for i in range(GROUP)]
        for h in group:
            for kv in range(2):
                @pl.when(pos > 0)
                def _():
                    halo(0, kv, h).wait_recv()

                @pl.when(pos < last)
                def _():
                    halo(1, kv, h).wait_recv()
        for p in range(pairs):
            r = pl.ds(p * PAIR, PAIR)
            w = pl.ds(p * PAIR, WINDOW)
            squares, products = sq[r, :], inner[r, :]
            for h in group:
                c = cols(h)
                scores = dot(kext[w, c], q[r, c], NT) * scale
                total = None
                for strand, kept in ((0, w1s), (1, w2s)):
                    s = scores + bias[strand, p]
                    e = jnp.exp(s - jnp.max(s, axis=0, keepdims=True))
                    e = e * (1.0 / jnp.sum(e, axis=0, keepdims=True))
                    kept[h, p] = e
                    total = e if total is None else total + e
                m = dot(total.astype(jnp.bfloat16), vext[w, c], TN)
                mixed[r, c] = m
                squares = squares + m * m
                products = products + gain_ref[pl.ds(h, 1), :] * og[r, c].astype(jnp.float32) * m
            sq[r, :] = squares
            inner[r, :] = products
        return carry

    lax.fori_loop(0, heads // GROUP, forward, 0)

    for p in range(pairs):
        r = slice(p * PAIR, (p + 1) * PAIR)
        sall[me_h, p : p + 1, :] = jnp.sum(sq[r, :].T, axis=0, keepdims=True)
        sall[me_h, pairs + p : pairs + p + 1, :] = jnp.sum(inner[r, :].T, axis=0, keepdims=True)

    def stat(slot, o, to):
        return pltpu.make_async_remote_copy(
            src_ref=sall.at[slot], dst_ref=sall.at[slot],
            send_sem=ssend.at[o], recv_sem=srecv.at[slot],
            device_id=(pos, to), device_id_type=MESH,
        )

    for o in range(1, n_head):
        stat(me_h, o, lax.rem(me_h + o, n_head)).start()
    for o in range(1, n_head):
        stat(lax.rem(me_h + o, n_head), o, me_h).wait_recv()
    tot = sall[0]
    for s in range(1, n_head):
        tot = tot + sall[s]
    inv = 1.0 / jnp.sqrt(tot[0:pairs] / width + 1e-06)
    coef = tot[pairs : 2 * pairs] / width * (inv * inv * inv)
    for p in range(pairs):
        r = slice(p * PAIR, (p + 1) * PAIR)
        invs[r, :] = jnp.broadcast_to(inv[p : p + 1], (PAIR, D)).T
        coefs[r, :] = jnp.broadcast_to(coef[p : p + 1], (PAIR, D)).T

    def normalise(h, carry):
        c = cols(h)
        gain = gain_ref[pl.ds(h, 1), :]
        m = mixed[:, c]
        g = og[:, c].astype(jnp.float32)
        iv = invs[...]
        mi = m * iv
        normed[:, c] = (gain * mi).astype(jnp.bfloat16)
        grad[:, c] = (gain * g * iv - m * coefs[...]).astype(jnp.bfloat16)
        gall[pos, pl.ds(h, 1), :] = jnp.sum(g * mi, axis=0, keepdims=True)
        return carry

    lax.fori_loop(0, heads, normalise, 0)

    def share(slot, o, to):
        return pltpu.make_async_remote_copy(
            src_ref=gall.at[slot], dst_ref=gall.at[slot],
            send_sem=gsend.at[o], recv_sem=grecv.at[slot],
            device_id=(to, me_h), device_id_type=MESH,
        )

    for o in range(1, n_ctx):
        share(pos, o, lax.rem(pos + o, n_ctx)).start()
    out_copies = [pltpu.make_async_copy(normed, normed_hbm, store_sem.at[0])]
    out_copies[0].start()

    def back(way, kv, h):
        return pltpu.make_async_remote_copy(
            src_ref=out_halo.at[way, kv, :, cols(h)],
            dst_ref=in_halo.at[way, kv, :, cols(h)],
            send_sem=bsend.at[way, kv, h],
            recv_sem=brecv.at[way, kv, h],
            device_id=((right, left)[way], me_h),
            device_id_type=MESH,
        )

    def backward(step, carry):
        group = [step * GROUP + i for i in range(GROUP)]
        for h in group:
            c = cols(h)
            parts = []
            for p in range(pairs):
                r = pl.ds(p * PAIR, PAIR)
                w = pl.ds(p * PAIR, WINDOW)
                g = grad[r, c]
                w1, w2 = w1s[h, p], w2s[h, p]
                wg = dot(vext[w, c], g, NT)
                c1 = jnp.sum(w1 * wg, axis=0, keepdims=True)
                c2 = jnp.sum(w2 * wg, axis=0, keepdims=True)
                ds = ((w1 * (wg - c1) + w2 * (wg - c2)) * scale).astype(jnp.bfloat16)
                dvw = dot((w1 + w2).astype(jnp.bfloat16), g, NN)
                dkw = dot(ds, q[r, c], NN)
                dq[r, c] = dot(ds, kext[w, c], TN).astype(jnp.bfloat16)
                parts.append((dkw, dvw))
            for kv, own in ((0, dk), (1, dv)):
                out_halo[1, kv, :, c] = parts[0][kv][0:RIM].astype(jnp.bfloat16)
                out_halo[0, kv, :, c] = parts[-1][kv][WINDOW - RIM :].astype(jnp.bfloat16)
                for p in range(pairs):
                    mid = parts[p][kv][RIM : RIM + PAIR]
                    if p > 0:
                        mid = mid + parts[p - 1][kv][RIM + PAIR :]
                    if p < pairs - 1:
                        mid = mid + parts[p + 1][kv][0:RIM]
                    own[pl.ds(p * PAIR, PAIR), c] = mid
        for h in group:
            for kv in range(2):
                @pl.when(pos < last)
                def _():
                    back(0, kv, h).start()

                @pl.when(pos > 0)
                def _():
                    back(1, kv, h).start()
        return carry

    lax.fori_loop(0, heads // GROUP, backward, 0)
    dq_copy = pltpu.make_async_copy(dq, dq_hbm, store_sem.at[1])
    dq_copy.start()
    out_copies.append(dq_copy)

    for o in range(1, n_ctx):
        share(lax.rem(pos + o, n_ctx), o, pos).wait_recv()
    total = gall[0]
    for s in range(1, n_ctx):
        total = total + gall[s]
    gg_ref[...] = total / math.sqrt(rows * n_ctx)

    @pl.when(pos == 0)
    def _():
        in_halo[0] = jnp.zeros(in_halo.shape[1:], in_halo.dtype)

    @pl.when(pos == last)
    def _():
        in_halo[1] = jnp.zeros(in_halo.shape[1:], in_halo.dtype)

    def settle(h, carry):
        c = cols(h)
        for kv, own, out in ((0, dk, dko), (1, dv, dvo)):
            @pl.when(pos > 0)
            def _():
                back(0, kv, h).wait_recv()

            @pl.when(pos < last)
            def _():
                back(1, kv, h).wait_recv()
            out[0:RIM, c] = (own[0:RIM, c] + in_halo[0, kv, :, c].astype(jnp.float32)).astype(jnp.bfloat16)
            out[rows - RIM : rows, c] = (
                own[rows - RIM : rows, c] + in_halo[1, kv, :, c].astype(jnp.float32)
            ).astype(jnp.bfloat16)
        return carry

    lax.fori_loop(0, heads, settle, 0)
    for i, (src, dst) in enumerate(((dko, dk_hbm), (dvo, dv_hbm))):
        copy = pltpu.make_async_copy(src, dst, store_sem.at[2 + i])
        copy.start()
        out_copies.append(copy)

    mirror.wait_send()
    for o in range(1, n_head):
        stat(me_h, o, lax.rem(me_h + o, n_head)).wait_send()
    for o in range(1, n_ctx):
        share(pos, o, lax.rem(pos + o, n_ctx)).wait_send()

    def drain(h, carry):
        for kv in range(2):
            @pl.when(pos < last)
            def _():
                halo(0, kv, h).wait_send()
                back(0, kv, h).wait_send()

            @pl.when(pos > 0)
            def _():
                halo(1, kv, h).wait_send()
                back(1, kv, h).wait_send()
        return carry

    lax.fori_loop(0, heads, drain, 0)
    for copy in out_copies:
        copy.wait()


def store_kernel(*refs):
    count = (len(refs) - 2) // 3
    ins, outs, held = refs[:count], refs[count : 2 * count], refs[2 * count : 3 * count]
    load_sem, store_sem = refs[3 * count :]
    loads = [pltpu.make_async_copy(ins[i], held[i], load_sem.at[i]) for i in range(count)]
    stores = [pltpu.make_async_copy(held[i], outs[i], store_sem.at[i]) for i in range(count)]
    for copy in loads:
        copy.start()
    for load, store in zip(loads, stores):
        load.wait()
        store.start()
    for copy in stores:
        copy.wait()


def body(query_vecs, key_vecs, value_vecs, out_grad, block_mask, norm_gain):
    n_ctx = lax.axis_size("ctx")
    n_head = lax.axis_size("head")
    rows, features = query_vecs.shape
    heads = features // D
    pairs = rows // PAIR
    ext = rows + 2 * RIM
    bf, f32 = jnp.bfloat16, jnp.float32
    dma = pltpu.SemaphoreType.DMA
    hbm = pl.BlockSpec(memory_space=pl.ANY)
    vmem = pl.BlockSpec(memory_space=pltpu.VMEM)
    fixed = pl.BlockSpec(memory_space=pltpu.HBM)
    big = jax.ShapeDtypeStruct((rows, features), bf)
    results = pl.pallas_call(
        functools.partial(kernel, n_ctx, n_head),
        out_shape=(big, big, big, big, jax.ShapeDtypeStruct((heads, D), f32)),
        in_specs=[fixed] * 6,
        out_specs=(hbm, hbm, hbm, hbm, vmem),
        scratch_shapes=[
            pltpu.VMEM(block_mask.shape, jnp.int32),
            pltpu.VMEM(norm_gain.shape, f32),
            pltpu.VMEM((rows, features), bf),
            pltpu.VMEM((ext, features), bf),
            pltpu.VMEM((ext, features), bf),
            pltpu.VMEM((rows, features), bf),
            pltpu.VMEM((8, 128), jnp.int32),
            pltpu.VMEM((8, 128), jnp.int32),
            pltpu.VMEM((2, pairs, WINDOW, PAIR), f32),
            pltpu.VMEM((heads, pairs, WINDOW, PAIR), f32),
            pltpu.VMEM((heads, pairs, WINDOW, PAIR), f32),
            pltpu.VMEM((rows, features), f32),
            pltpu.VMEM((rows, D), f32),
            pltpu.VMEM((rows, D), f32),
            pltpu.VMEM((n_head, 8, PAIR), f32),
            pltpu.VMEM((rows, D), f32),
            pltpu.VMEM((rows, D), f32),
            pltpu.VMEM((rows, features), bf),
            pltpu.VMEM((n_ctx, heads, D), f32),
            pltpu.VMEM((rows, features), bf),
            pltpu.VMEM((rows, features), bf),
            pltpu.VMEM((rows, features), f32),
            pltpu.VMEM((rows, features), f32),
            pltpu.VMEM((rows, features), bf),
            pltpu.VMEM((rows, features), bf),
            pltpu.VMEM((2, 2, RIM, features), bf),
            pltpu.VMEM((2, 2, RIM, features), bf),
            dma((6,)),
            dma((2, 2, heads)),
            dma((2, 2, heads)),
            dma,
            dma,
            dma((n_head,)),
            dma((n_head,)),
            dma((n_ctx,)),
            dma((n_ctx,)),
            dma((2, 2, heads)),
            dma((2, 2, heads)),
            dma((4,)),
        ],
        compiler_params=pltpu.CompilerParams(
            collective_id=0, has_side_effects=True, vmem_limit_bytes=VMEM
        ),
        name="strand_attention",
    )(query_vecs, key_vecs, value_vecs, out_grad, block_mask, norm_gain)
    return pl.pallas_call(
        store_kernel,
        out_shape=tuple(jax.ShapeDtypeStruct(x.shape, x.dtype) for x in results),
        in_specs=[hbm] * 5,
        out_specs=(fixed,) * 5,
        scratch_shapes=[pltpu.VMEM(x.shape, x.dtype) for x in results] + [dma((5,)), dma((5,))],
        compiler_params=pltpu.CompilerParams(vmem_limit_bytes=VMEM),
        name="store_results",
    )(*results)


def solution(mesh):
    tokens = P("ctx", "head")
    return jax.shard_map(
        body,
        mesh=mesh,
        in_specs=(tokens, tokens, tokens, tokens, P("ctx", None), P("head", None)),
        out_specs=(tokens, tokens, tokens, tokens, P("head", None)),
        check_vma=False,
    )
```

```python
import functools
import math

import jax
import jax.numpy as jnp
from jax import lax
from jax.experimental import pallas as pl
from jax.experimental.pallas import tpu as pltpu
from jax.sharding import PartitionSpec as P

D = 128
BLOCK = 64
BAND = 2
RIM = BAND * BLOCK
PAIR = 2 * BLOCK
WINDOW = PAIR + 2 * RIM
VMEM = 64 * 1024 * 1024
GROUP = 2
MESH = pl.DeviceIdType.MESH
NT = (((1,), (1,)), ((), ()))
TN = (((0,), (0,)), ((), ()))
NN = (((1,), (0,)), ((), ()))


def dot(a, b, dims):
    return lax.dot_general(a, b, dims, preferred_element_type=jnp.float32)


def kernel(
    n_ctx, n_head,
    q_hbm, k_hbm, v_hbm, og_hbm, mask_hbm, gain_hbm,
    normed_hbm, dq_hbm, dk_hbm, dv_hbm, gg_ref,
    mask_ref, gain_ref, q, kext, vext, og, mine, theirs, bias, w1s, w2s, mixed, sq, inner, sall, invs, coefs,
    grad, gall, normed, dq, dk, dv, dko, dvo, out_halo, in_halo,
    load_sem, fsend, frecv, msend, mrecv, ssend, srecv, gsend, grecv, bsend, brecv, store_sem, relay, asend, rsend, rrecv,
):
    pos = lax.axis_index("ctx")
    me_h = lax.axis_index("head")
    rows, features = q.shape
    heads = features // D
    pairs = rows // PAIR
    blocks_dev = rows // BLOCK
    width = features * n_head
    scale = D ** -0.5
    last = n_ctx - 1

    small = [
        pltpu.make_async_copy(mask_hbm, mask_ref, load_sem.at[4]),
        pltpu.make_async_copy(gain_hbm, gain_ref, load_sem.at[5]),
    ]
    loads = [
        pltpu.make_async_copy(k_hbm, kext.at[pl.ds(RIM, rows)], load_sem.at[0]),
        pltpu.make_async_copy(q_hbm, q, load_sem.at[1]),
        pltpu.make_async_copy(v_hbm, vext.at[pl.ds(RIM, rows)], load_sem.at[2]),
        pltpu.make_async_copy(og_hbm, og, load_sem.at[3]),
    ]
    for copy in small + loads:
        copy.start()

    barrier = pltpu.get_barrier_semaphore()
    for o in range(1, n_ctx):
        pl.semaphore_signal(barrier, inc=1, device_id=(lax.rem(pos + o, n_ctx), me_h), device_id_type=MESH)
    for o in range(1, n_head):
        pl.semaphore_signal(barrier, inc=1, device_id=(pos, lax.rem(me_h + o, n_head)), device_id_type=MESH)
    mine[...] = jnp.zeros_like(mine)
    for copy in small:
        copy.wait()
    mine[0:blocks_dev, 0:mask_ref.shape[1]] = mask_ref[...]
    sall[me_h] = jnp.zeros(sall.shape[1:], jnp.float32)
    sq[...] = jnp.zeros_like(sq)
    inner[...] = jnp.zeros_like(inner)

    @pl.when(pos == 0)
    def _():
        kext[0:RIM, :] = jnp.zeros((RIM, features), kext.dtype)
        vext[0:RIM, :] = jnp.zeros((RIM, features), vext.dtype)

    @pl.when(pos == last)
    def _():
        kext[rows + RIM :, :] = jnp.zeros((RIM, features), kext.dtype)
        vext[rows + RIM :, :] = jnp.zeros((RIM, features), vext.dtype)

    pl.semaphore_wait(barrier, n_ctx - 1 + n_head - 1)

    def cols(h):
        return pl.ds(pl.multiple_of(h * D, D), D)

    right = jnp.minimum(pos + 1, last)
    left = jnp.maximum(pos - 1, 0)

    square = n_ctx == 8
    ends = (n_ctx // 2 - 1, n_ctx // 2)
    corners = (last, 0)

    def first_leg(way, phase, kv, step):
        h = step * GROUP + 1
        if phase == 0:
            src = (k_hbm, v_hbm)[kv].at[pl.ds((rows - RIM, 0)[way], RIM), cols(h)]
        else:
            src = out_halo.at[way, kv, :, cols(h)]
        return pltpu.make_async_remote_copy(
            src_ref=src, dst_ref=relay.at[phase, kv, step],
            send_sem=asend.at[phase, kv, step], recv_sem=rrecv.at[phase, kv, step],
            device_id=(corners[way], me_h), device_id_type=MESH,
        )

    def second_leg(way, phase, kv, step):
        h = step * GROUP + 1
        if phase == 0:
            dst = (kext, vext)[kv].at[pl.ds((0, rows + RIM)[way], RIM), cols(h)]
            sem = frecv.at[way, kv, h]
        else:
            dst = in_halo.at[way, kv, :, cols(h)]
            sem = brecv.at[way, kv, h]
        return pltpu.make_async_remote_copy(
            src_ref=relay.at[phase, kv, step], dst_ref=dst,
            send_sem=rsend.at[phase, kv, step], recv_sem=sem,
            device_id=(ends[1 - way], me_h), device_id_type=MESH,
        )

    def pass_on(phase, step):
        if square:
            for way in range(2):
                @pl.when(pos == corners[way])
                def _():
                    for kv in range(2):
                        first_leg(way, phase, kv, step).wait_recv()
                        second_leg(way, phase, kv, step).start()

    def each_send(phase, step, plain, act):
        for i in range(GROUP):
            h = step * GROUP + i
            for kv in range(2):
                for way in range(2):
                    able = (pos < last, pos > 0)[way]
                    if square and i == 1:
                        @pl.when(pos == ends[way])
                        def _():
                            act(first_leg(way, phase, kv, step))

                        able = able & (pos != ends[way])

                    @pl.when(able)
                    def _():
                        act(plain(way, kv, h))

    def halo(way, kv, h):
        src = (k_hbm, v_hbm)[kv]
        dst = (kext, vext)[kv]
        from_row, to_row = ((rows - RIM, 0), (0, rows + RIM))[way]
        return pltpu.make_async_remote_copy(
            src_ref=src.at[pl.ds(from_row, RIM), cols(h)],
            dst_ref=dst.at[pl.ds(to_row, RIM), cols(h)],
            send_sem=fsend.at[way, kv, h],
            recv_sem=frecv.at[way, kv, h],
            device_id=((right, left)[way], me_h),
            device_id_type=MESH,
        )

    mirror = pltpu.make_async_remote_copy(
        src_ref=mine, dst_ref=theirs, send_sem=msend, recv_sem=mrecv,
        device_id=(last - pos, me_h), device_id_type=MESH,
    )
    mirror.start()

    def send_halos(step, carry):
        each_send(0, step, halo, lambda copy: copy.start())
        return carry

    lax.fori_loop(0, heads // GROUP, send_halos, 0)
    mirror.wait_recv()

    all_blocks = blocks_dev * n_ctx
    row_block = lax.broadcasted_iota(jnp.int32, (WINDOW, PAIR), 0) // BLOCK
    second = lax.broadcasted_iota(jnp.int32, (8, PAIR), 1) >= BLOCK
    for strand in range(2):
        table = (mine, theirs)[strand]
        for p in range(pairs):
            first = pos * blocks_dev - BAND + 2 * p
            live = None
            for n in range(mask_ref.shape[1]):
                lists = []
                for b in (2 * p, 2 * p + 1):
                    r = b if strand == 0 else blocks_dev - 1 - b
                    lists.append(jnp.broadcast_to(table[r : r + 1, n : n + 1], (8, PAIR)))
                entry = jnp.where(second, lists[1], lists[0])
                if strand == 1:
                    target = all_blocks - 1 - entry
                else:
                    target = entry
                target = jnp.where(entry >= 0, target - first, -1)[0:1]
                hit = row_block == target
                live = hit if live is None else live | hit
            bias[strand, p] = jnp.where(live, 0.0, -1e30)

    for copy in loads:
        copy.wait()

    def forward(step, carry):
        group = [step * GROUP + i for i in range(GROUP)]
        pass_on(0, step)
        for h in group:
            for kv in range(2):
                @pl.when(pos > 0)
                def _():
                    halo(0, kv, h).wait_recv()

                @pl.when(pos < last)
                def _():
                    halo(1, kv, h).wait_recv()
        for p in range(pairs):
            r = pl.ds(p * PAIR, PAIR)
            w = pl.ds(p * PAIR, WINDOW)
            squares, products = sq[r, :], inner[r, :]
            for h in group:
                c = cols(h)
                scores = dot(kext[w, c], q[r, c], NT) * scale
                total = None
                for strand, kept in ((0, w1s), (1, w2s)):
                    s = scores + bias[strand, p]
                    e = jnp.exp(s - jnp.max(s, axis=0, keepdims=True))
                    e = e * (1.0 / jnp.sum(e, axis=0, keepdims=True))
                    kept[h, p] = e
                    total = e if total is None else total + e
                m = dot(total.astype(jnp.bfloat16), vext[w, c], TN)
                mixed[r, c] = m
                squares = squares + m * m
                products = products + gain_ref[pl.ds(h, 1), :] * og[r, c].astype(jnp.float32) * m
            sq[r, :] = squares
            inner[r, :] = products
        return carry

    lax.fori_loop(0, heads // GROUP, forward, 0)

    for p in range(pairs):
        r = slice(p * PAIR, (p + 1) * PAIR)
        sall[me_h, p : p + 1, :] = jnp.sum(sq[r, :].T, axis=0, keepdims=True)
        sall[me_h, pairs + p : pairs + p + 1, :] = jnp.sum(inner[r, :].T, axis=0, keepdims=True)

    def stat(slot, o, to):
        return pltpu.make_async_remote_copy(
            src_ref=sall.at[slot], dst_ref=sall.at[slot],
            send_sem=ssend.at[o], recv_sem=srecv.at[slot],
            device_id=(pos, to), device_id_type=MESH,
        )

    for o in range(1, n_head):
        stat(me_h, o, lax.rem(me_h + o, n_head)).start()
    for o in range(1, n_head):
        stat(lax.rem(me_h + o, n_head), o, me_h).wait_recv()
    tot = sall[0]
    for s in range(1, n_head):
        tot = tot + sall[s]
    inv = 1.0 / jnp.sqrt(tot[0:pairs] / width + 1e-06)
    coef = tot[pairs : 2 * pairs] / width * (inv * inv * inv)
    for p in range(pairs):
        r = slice(p * PAIR, (p + 1) * PAIR)
        invs[r, :] = jnp.broadcast_to(inv[p : p + 1], (PAIR, D)).T
        coefs[r, :] = jnp.broadcast_to(coef[p : p + 1], (PAIR, D)).T

    def normalise(h, carry):
        c = cols(h)
        gain = gain_ref[pl.ds(h, 1), :]
        m = mixed[:, c]
        g = og[:, c].astype(jnp.float32)
        iv = invs[...]
        mi = m * iv
        normed[:, c] = (gain * mi).astype(jnp.bfloat16)
        grad[:, c] = (gain * g * iv - m * coefs[...]).astype(jnp.bfloat16)
        gall[pos, pl.ds(h, 1), :] = jnp.sum(g * mi, axis=0, keepdims=True)
        return carry

    lax.fori_loop(0, heads, normalise, 0)

    def share(slot, o, to):
        return pltpu.make_async_remote_copy(
            src_ref=gall.at[slot], dst_ref=gall.at[slot],
            send_sem=gsend.at[o], recv_sem=grecv.at[slot],
            device_id=(to, me_h), device_id_type=MESH,
        )

    for o in range(1, n_ctx):
        share(pos, o, lax.rem(pos + o, n_ctx)).start()
    out_copies = [pltpu.make_async_copy(normed, normed_hbm, store_sem.at[0])]
    out_copies[0].start()

    def back(way, kv, h):
        return pltpu.make_async_remote_copy(
            src_ref=out_halo.at[way, kv, :, cols(h)],
            dst_ref=in_halo.at[way, kv, :, cols(h)],
            send_sem=bsend.at[way, kv, h],
            recv_sem=brecv.at[way, kv, h],
            device_id=((right, left)[way], me_h),
            device_id_type=MESH,
        )

    def backward(step, carry):
        group = [step * GROUP + i for i in range(GROUP)]
        for h in group:
            c = cols(h)
            parts = []
            for p in range(pairs):
                r = pl.ds(p * PAIR, PAIR)
                w = pl.ds(p * PAIR, WINDOW)
                g = grad[r, c]
                w1, w2 = w1s[h, p], w2s[h, p]
                wg = dot(vext[w, c], g, NT)
                c1 = jnp.sum(w1 * wg, axis=0, keepdims=True)
                c2 = jnp.sum(w2 * wg, axis=0, keepdims=True)
                ds = ((w1 * (wg - c1) + w2 * (wg - c2)) * scale).astype(jnp.bfloat16)
                dvw = dot((w1 + w2).astype(jnp.bfloat16), g, NN)
                dkw = dot(ds, q[r, c], NN)
                dq[r, c] = dot(ds, kext[w, c], TN).astype(jnp.bfloat16)
                parts.append((dkw, dvw))
            for kv, own in ((0, dk), (1, dv)):
                out_halo[1, kv, :, c] = parts[0][kv][0:RIM].astype(jnp.bfloat16)
                out_halo[0, kv, :, c] = parts[-1][kv][WINDOW - RIM :].astype(jnp.bfloat16)
                for p in range(pairs):
                    mid = parts[p][kv][RIM : RIM + PAIR]
                    if p > 0:
                        mid = mid + parts[p - 1][kv][RIM + PAIR :]
                    if p < pairs - 1:
                        mid = mid + parts[p + 1][kv][0:RIM]
                    own[pl.ds(p * PAIR, PAIR), c] = mid
        each_send(1, step, back, lambda copy: copy.start())

        @pl.when(step > 0)
        def _():
            pass_on(1, step - 1)

        return carry

    lax.fori_loop(0, heads // GROUP, backward, 0)
    pass_on(1, heads // GROUP - 1)
    dq_copy = pltpu.make_async_copy(dq, dq_hbm, store_sem.at[1])
    dq_copy.start()
    out_copies.append(dq_copy)

    for o in range(1, n_ctx):
        share(lax.rem(pos + o, n_ctx), o, pos).wait_recv()
    total = gall[0]
    for s in range(1, n_ctx):
        total = total + gall[s]
    gg_ref[...] = total / math.sqrt(rows * n_ctx)

    @pl.when(pos == 0)
    def _():
        in_halo[0] = jnp.zeros(in_halo.shape[1:], in_halo.dtype)

    @pl.when(pos == last)
    def _():
        in_halo[1] = jnp.zeros(in_halo.shape[1:], in_halo.dtype)

    def settle(h, carry):
        c = cols(h)
        for kv, own, out in ((0, dk, dko), (1, dv, dvo)):
            @pl.when(pos > 0)
            def _():
                back(0, kv, h).wait_recv()

            @pl.when(pos < last)
            def _():
                back(1, kv, h).wait_recv()
            out[0:RIM, c] = (own[0:RIM, c] + in_halo[0, kv, :, c].astype(jnp.float32)).astype(jnp.bfloat16)
            out[rows - RIM : rows, c] = (
                own[rows - RIM : rows, c] + in_halo[1, kv, :, c].astype(jnp.float32)
            ).astype(jnp.bfloat16)
        return carry

    lax.fori_loop(0, heads, settle, 0)
    for i, (src, dst) in enumerate(((dko, dk_hbm), (dvo, dv_hbm))):
        copy = pltpu.make_async_copy(src, dst, store_sem.at[2 + i])
        copy.start()
        out_copies.append(copy)

    mirror.wait_send()
    for o in range(1, n_head):
        stat(me_h, o, lax.rem(me_h + o, n_head)).wait_send()
    for o in range(1, n_ctx):
        share(pos, o, lax.rem(pos + o, n_ctx)).wait_send()

    def drain(step, carry):
        for phase, plain in ((0, halo), (1, back)):
            each_send(phase, step, plain, lambda copy: copy.wait_send())
            if square:
                for way in range(2):
                    @pl.when(pos == corners[way])
                    def _():
                        for kv in range(2):
                            second_leg(way, phase, kv, step).wait_send()
        return carry

    lax.fori_loop(0, heads // GROUP, drain, 0)
    for copy in out_copies:
        copy.wait()


def store_kernel(*refs):
    count = (len(refs) - 2) // 3
    ins, outs, held = refs[:count], refs[count : 2 * count], refs[2 * count : 3 * count]
    load_sem, store_sem = refs[3 * count :]
    loads = [pltpu.make_async_copy(ins[i], held[i], load_sem.at[i]) for i in range(count)]
    stores = [pltpu.make_async_copy(held[i], outs[i], store_sem.at[i]) for i in range(count)]
    for copy in loads:
        copy.start()
    for load, store in zip(loads, stores):
        load.wait()
        store.start()
    for copy in stores:
        copy.wait()


def body(query_vecs, key_vecs, value_vecs, out_grad, block_mask, norm_gain):
    n_ctx = lax.axis_size("ctx")
    n_head = lax.axis_size("head")
    rows, features = query_vecs.shape
    heads = features // D
    pairs = rows // PAIR
    ext = rows + 2 * RIM
    bf, f32 = jnp.bfloat16, jnp.float32
    dma = pltpu.SemaphoreType.DMA
    hbm = pl.BlockSpec(memory_space=pl.ANY)
    vmem = pl.BlockSpec(memory_space=pltpu.VMEM)
    fixed = pl.BlockSpec(memory_space=pltpu.HBM)
    big = jax.ShapeDtypeStruct((rows, features), bf)
    results = pl.pallas_call(
        functools.partial(kernel, n_ctx, n_head),
        out_shape=(big, big, big, big, jax.ShapeDtypeStruct((heads, D), f32)),
        in_specs=[fixed] * 6,
        out_specs=(hbm, hbm, hbm, hbm, vmem),
        scratch_shapes=[
            pltpu.VMEM(block_mask.shape, jnp.int32),
            pltpu.VMEM(norm_gain.shape, f32),
            pltpu.VMEM((rows, features), bf),
            pltpu.VMEM((ext, features), bf),
            pltpu.VMEM((ext, features), bf),
            pltpu.VMEM((rows, features), bf),
            pltpu.VMEM((8, 128), jnp.int32),
            pltpu.VMEM((8, 128), jnp.int32),
            pltpu.VMEM((2, pairs, WINDOW, PAIR), f32),
            pltpu.VMEM((heads, pairs, WINDOW, PAIR), f32),
            pltpu.VMEM((heads, pairs, WINDOW, PAIR), f32),
            pltpu.VMEM((rows, features), f32),
            pltpu.VMEM((rows, D), f32),
            pltpu.VMEM((rows, D), f32),
            pltpu.VMEM((n_head, 8, PAIR), f32),
            pltpu.VMEM((rows, D), f32),
            pltpu.VMEM((rows, D), f32),
            pltpu.VMEM((rows, features), bf),
            pltpu.VMEM((n_ctx, heads, D), f32),
            pltpu.VMEM((rows, features), bf),
            pltpu.VMEM((rows, features), bf),
            pltpu.VMEM((rows, features), f32),
            pltpu.VMEM((rows, features), f32),
            pltpu.VMEM((rows, features), bf),
            pltpu.VMEM((rows, features), bf),
            pltpu.VMEM((2, 2, RIM, features), bf),
            pltpu.VMEM((2, 2, RIM, features), bf),
            dma((6,)),
            dma((2, 2, heads)),
            dma((2, 2, heads)),
            dma,
            dma,
            dma((n_head,)),
            dma((n_head,)),
            dma((n_ctx,)),
            dma((n_ctx,)),
            dma((2, 2, heads)),
            dma((2, 2, heads)),
            dma((4,)),
            pltpu.VMEM((2, 2, heads // GROUP, RIM, D), bf),
            dma((2, 2, heads // GROUP)),
            dma((2, 2, heads // GROUP)),
            dma((2, 2, heads // GROUP)),
        ],
        compiler_params=pltpu.CompilerParams(
            collective_id=0, has_side_effects=True, vmem_limit_bytes=VMEM
        ),
        name="strand_attention",
    )(query_vecs, key_vecs, value_vecs, out_grad, block_mask, norm_gain)
    return pl.pallas_call(
        store_kernel,
        out_shape=tuple(jax.ShapeDtypeStruct(x.shape, x.dtype) for x in results),
        in_specs=[hbm] * 5,
        out_specs=(fixed,) * 5,
        scratch_shapes=[pltpu.VMEM(x.shape, x.dtype) for x in results] + [dma((5,)), dma((5,))],
        compiler_params=pltpu.CompilerParams(vmem_limit_bytes=VMEM),
        name="store_results",
    )(*results)


def solution(mesh):
    tokens = P("ctx", "head")
    return jax.shard_map(
        body,
        mesh=mesh,
        in_specs=(tokens, tokens, tokens, tokens, P("ctx", None), P("head", None)),
        out_specs=(tokens, tokens, tokens, tokens, P("head", None)),
        check_vma=False,
    )
```

```python
import functools
import math

import jax
import jax.numpy as jnp
from jax import lax
from jax.experimental import pallas as pl
from jax.experimental.pallas import tpu as pltpu
from jax.sharding import PartitionSpec as P

D = 128
BLOCK = 64
BAND = 2
RIM = BAND * BLOCK
PAIR = 2 * BLOCK
WINDOW = PAIR + 2 * RIM
VMEM = 64 * 1024 * 1024
GROUP = 2
MESH = pl.DeviceIdType.MESH
NT = (((1,), (1,)), ((), ()))
TN = (((0,), (0,)), ((), ()))
NN = (((1,), (0,)), ((), ()))


def dot(a, b, dims):
    return lax.dot_general(a, b, dims, preferred_element_type=jnp.float32)


def kernel(
    n_ctx, n_head,
    q_hbm, k_hbm, v_hbm, og_hbm, mask_hbm, gain_hbm,
    normed_hbm, dq_hbm, dk_hbm, dv_hbm, gg_ref,
    mask_ref, gain_ref, q, kvext, og, mine, theirs, bias, w1s, w2s, mixed, sq, inner, sall, invs, coefs,
    grad, gall, normed, dq, dk, dv, dko, dvo, out_halo, in_halo,
    load_sem, fsend, frecv, msend, mrecv, ssend, srecv, gsend, grecv, bsend, brecv, store_sem, kv_sem,
):
    pos = lax.axis_index("ctx")
    me_h = lax.axis_index("head")
    rows, features = q.shape
    heads = features // D
    pairs = rows // PAIR
    blocks_dev = rows // BLOCK
    width = features * n_head
    scale = D ** -0.5
    last = n_ctx - 1

    small = [
        pltpu.make_async_copy(mask_hbm, mask_ref, load_sem.at[2]),
        pltpu.make_async_copy(gain_hbm, gain_ref, load_sem.at[3]),
    ]
    def cols(h):
        return pl.ds(pl.multiple_of(h * D, D), D)

    def head_load(kv, h):
        return pltpu.make_async_copy(
            (k_hbm, v_hbm)[kv].at[:, cols(h)], kvext.at[h, kv, pl.ds(RIM, rows)], kv_sem.at[kv, h]
        )

    loads = [
        pltpu.make_async_copy(q_hbm, q, load_sem.at[0]),
        pltpu.make_async_copy(og_hbm, og, load_sem.at[1]),
    ]
    kv_loads = [head_load(kv, h) for h in range(heads) for kv in range(2)]
    for copy in small + kv_loads + loads:
        copy.start()

    barrier = pltpu.get_barrier_semaphore()
    for o in range(1, n_ctx):
        pl.semaphore_signal(barrier, inc=1, device_id=(lax.rem(pos + o, n_ctx), me_h), device_id_type=MESH)
    for o in range(1, n_head):
        pl.semaphore_signal(barrier, inc=1, device_id=(pos, lax.rem(me_h + o, n_head)), device_id_type=MESH)
    mine[...] = jnp.zeros_like(mine)
    for copy in small:
        copy.wait()
    mine[0:blocks_dev, 0:mask_ref.shape[1]] = mask_ref[...]
    sall[me_h] = jnp.zeros(sall.shape[1:], jnp.float32)
    sq[...] = jnp.zeros_like(sq)
    inner[...] = jnp.zeros_like(inner)

    @pl.when(pos == 0)
    def _():
        kvext[:, :, 0:RIM, :] = jnp.zeros((heads, 2, RIM, D), kvext.dtype)

    @pl.when(pos == last)
    def _():
        kvext[:, :, rows + RIM :, :] = jnp.zeros((heads, 2, RIM, D), kvext.dtype)

    pl.semaphore_wait(barrier, n_ctx - 1 + n_head - 1)

    right = jnp.minimum(pos + 1, last)
    left = jnp.maximum(pos - 1, 0)

    def halo(way, h):
        from_row, to_row = ((rows, 0), (RIM, rows + RIM))[way]
        return pltpu.make_async_remote_copy(
            src_ref=kvext.at[h, :, pl.ds(from_row, RIM)],
            dst_ref=kvext.at[h, :, pl.ds(to_row, RIM)],
            send_sem=fsend.at[way, h],
            recv_sem=frecv.at[way, h],
            device_id=((right, left)[way], me_h),
            device_id_type=MESH,
        )

    mirror = pltpu.make_async_remote_copy(
        src_ref=mine, dst_ref=theirs, send_sem=msend, recv_sem=mrecv,
        device_id=(last - pos, me_h), device_id_type=MESH,
    )
    mirror.start()

    for copy in kv_loads:
        copy.wait()

    def each_way(act, plain, h):
        @pl.when(pos < last)
        def _():
            act(plain(0, h))

        @pl.when(pos > 0)
        def _():
            act(plain(1, h))

    def each_arrival(plain, h):
        @pl.when(pos > 0)
        def _():
            plain(0, h).wait_recv()

        @pl.when(pos < last)
        def _():
            plain(1, h).wait_recv()

    for h in range(heads):
        each_way(lambda copy: copy.start(), halo, h)
    mirror.wait_recv()

    all_blocks = blocks_dev * n_ctx
    row_block = lax.broadcasted_iota(jnp.int32, (WINDOW, PAIR), 0) // BLOCK
    second = lax.broadcasted_iota(jnp.int32, (8, PAIR), 1) >= BLOCK
    for strand in range(2):
        table = (mine, theirs)[strand]
        for p in range(pairs):
            first = pos * blocks_dev - BAND + 2 * p
            live = None
            for n in range(mask_ref.shape[1]):
                lists = []
                for b in (2 * p, 2 * p + 1):
                    r = b if strand == 0 else blocks_dev - 1 - b
                    lists.append(jnp.broadcast_to(table[r : r + 1, n : n + 1], (8, PAIR)))
                entry = jnp.where(second, lists[1], lists[0])
                if strand == 1:
                    target = all_blocks - 1 - entry
                else:
                    target = entry
                target = jnp.where(entry >= 0, target - first, -1)[0:1]
                hit = row_block == target
                live = hit if live is None else live | hit
            bias[strand, p] = jnp.where(live, 0.0, -1e30)

    for copy in loads:
        copy.wait()

    def forward(step, carry):
        group = [step * GROUP + i for i in range(GROUP)]
        for h in group:
            each_arrival(halo, h)
        for p in range(pairs):
            r = pl.ds(p * PAIR, PAIR)
            w = pl.ds(p * PAIR, WINDOW)
            squares, products = sq[r, :], inner[r, :]
            for h in group:
                c = cols(h)
                scores = dot(kvext[h, 0, w], q[r, c], NT) * scale
                total = None
                for strand, kept in ((0, w1s), (1, w2s)):
                    s = scores + bias[strand, p]
                    e = jnp.exp(s - jnp.max(s, axis=0, keepdims=True))
                    e = e * (1.0 / jnp.sum(e, axis=0, keepdims=True))
                    kept[h, p] = e
                    total = e if total is None else total + e
                m = dot(total.astype(jnp.bfloat16), kvext[h, 1, w], TN)
                mixed[r, c] = m
                squares = squares + m * m
                products = products + gain_ref[pl.ds(h, 1), :] * og[r, c].astype(jnp.float32) * m
            sq[r, :] = squares
            inner[r, :] = products
        return carry

    lax.fori_loop(0, heads // GROUP, forward, 0)

    for p in range(pairs):
        r = slice(p * PAIR, (p + 1) * PAIR)
        sall[me_h, p : p + 1, :] = jnp.sum(sq[r, :].T, axis=0, keepdims=True)
        sall[me_h, pairs + p : pairs + p + 1, :] = jnp.sum(inner[r, :].T, axis=0, keepdims=True)

    def stat(slot, o, to):
        return pltpu.make_async_remote_copy(
            src_ref=sall.at[slot], dst_ref=sall.at[slot],
            send_sem=ssend.at[o], recv_sem=srecv.at[slot],
            device_id=(pos, to), device_id_type=MESH,
        )

    for o in range(1, n_head):
        stat(me_h, o, lax.rem(me_h + o, n_head)).start()
    for o in range(1, n_head):
        stat(lax.rem(me_h + o, n_head), o, me_h).wait_recv()
    tot = sall[0]
    for s in range(1, n_head):
        tot = tot + sall[s]
    inv = 1.0 / jnp.sqrt(tot[0:pairs] / width + 1e-06)
    coef = tot[pairs : 2 * pairs] / width * (inv * inv * inv)
    for p in range(pairs):
        r = slice(p * PAIR, (p + 1) * PAIR)
        invs[r, :] = jnp.broadcast_to(inv[p : p + 1], (PAIR, D)).T
        coefs[r, :] = jnp.broadcast_to(coef[p : p + 1], (PAIR, D)).T

    def normalise(h, carry):
        c = cols(h)
        gain = gain_ref[pl.ds(h, 1), :]
        m = mixed[:, c]
        g = og[:, c].astype(jnp.float32)
        iv = invs[...]
        mi = m * iv
        normed[:, c] = (gain * mi).astype(jnp.bfloat16)
        grad[:, c] = (gain * g * iv - m * coefs[...]).astype(jnp.bfloat16)
        gall[pos, pl.ds(h, 1), :] = jnp.sum(g * mi, axis=0, keepdims=True)
        return carry

    lax.fori_loop(0, heads, normalise, 0)

    def share(slot, o, to):
        return pltpu.make_async_remote_copy(
            src_ref=gall.at[slot], dst_ref=gall.at[slot],
            send_sem=gsend.at[o], recv_sem=grecv.at[slot],
            device_id=(to, me_h), device_id_type=MESH,
        )

    for o in range(1, n_ctx):
        share(pos, o, lax.rem(pos + o, n_ctx)).start()
    out_copies = [pltpu.make_async_copy(normed, normed_hbm, store_sem.at[0])]
    out_copies[0].start()

    def back(way, h):
        return pltpu.make_async_remote_copy(
            src_ref=out_halo.at[way, h],
            dst_ref=in_halo.at[way, h],
            send_sem=bsend.at[way, h],
            recv_sem=brecv.at[way, h],
            device_id=((right, left)[way], me_h),
            device_id_type=MESH,
        )

    def backward(step, carry):
        group = [step * GROUP + i for i in range(GROUP)]
        for h in group:
            c = cols(h)
            parts = []
            for p in range(pairs):
                r = pl.ds(p * PAIR, PAIR)
                w = pl.ds(p * PAIR, WINDOW)
                g = grad[r, c]
                w1, w2 = w1s[h, p], w2s[h, p]
                wg = dot(kvext[h, 1, w], g, NT)
                c1 = jnp.sum(w1 * wg, axis=0, keepdims=True)
                c2 = jnp.sum(w2 * wg, axis=0, keepdims=True)
                ds = ((w1 * (wg - c1) + w2 * (wg - c2)) * scale).astype(jnp.bfloat16)
                dvw = dot((w1 + w2).astype(jnp.bfloat16), g, NN)
                dkw = dot(ds, q[r, c], NN)
                dq[r, c] = dot(ds, kvext[h, 0, w], TN).astype(jnp.bfloat16)
                parts.append((dkw, dvw))
            for kv, own in ((0, dk), (1, dv)):
                out_halo[1, h, kv] = parts[0][kv][0:RIM].astype(jnp.bfloat16)
                out_halo[0, h, kv] = parts[-1][kv][WINDOW - RIM :].astype(jnp.bfloat16)
                for p in range(pairs):
                    mid = parts[p][kv][RIM : RIM + PAIR]
                    if p > 0:
                        mid = mid + parts[p - 1][kv][RIM + PAIR :]
                    if p < pairs - 1:
                        mid = mid + parts[p + 1][kv][0:RIM]
                    own[pl.ds(p * PAIR, PAIR), c] = mid
        for h in group:
            each_way(lambda copy: copy.start(), back, h)
        return carry

    lax.fori_loop(0, heads // GROUP, backward, 0)
    dq_copy = pltpu.make_async_copy(dq, dq_hbm, store_sem.at[1])
    dq_copy.start()
    out_copies.append(dq_copy)

    for o in range(1, n_ctx):
        share(lax.rem(pos + o, n_ctx), o, pos).wait_recv()
    total = gall[0]
    for s in range(1, n_ctx):
        total = total + gall[s]
    gg_ref[...] = total / math.sqrt(rows * n_ctx)

    @pl.when(pos == 0)
    def _():
        in_halo[0] = jnp.zeros(in_halo.shape[1:], in_halo.dtype)

    @pl.when(pos == last)
    def _():
        in_halo[1] = jnp.zeros(in_halo.shape[1:], in_halo.dtype)

    def settle(h, carry):
        c = cols(h)
        each_arrival(back, h)
        for kv, own, out in ((0, dk, dko), (1, dv, dvo)):
            out[0:RIM, c] = (own[0:RIM, c] + in_halo[0, h, kv].astype(jnp.float32)).astype(jnp.bfloat16)
            out[rows - RIM : rows, c] = (
                own[rows - RIM : rows, c] + in_halo[1, h, kv].astype(jnp.float32)
            ).astype(jnp.bfloat16)
        return carry

    lax.fori_loop(0, heads, settle, 0)
    for i, (src, dst) in enumerate(((dko, dk_hbm), (dvo, dv_hbm))):
        copy = pltpu.make_async_copy(src, dst, store_sem.at[2 + i])
        copy.start()
        out_copies.append(copy)

    mirror.wait_send()
    for o in range(1, n_head):
        stat(me_h, o, lax.rem(me_h + o, n_head)).wait_send()
    for o in range(1, n_ctx):
        share(pos, o, lax.rem(pos + o, n_ctx)).wait_send()

    for h in range(heads):
        each_way(lambda copy: copy.wait_send(), halo, h)
        each_way(lambda copy: copy.wait_send(), back, h)
    for copy in out_copies:
        copy.wait()


def store_kernel(*refs):
    count = (len(refs) - 2) // 3
    ins, outs, held = refs[:count], refs[count : 2 * count], refs[2 * count : 3 * count]
    load_sem, store_sem = refs[3 * count :]
    loads = [pltpu.make_async_copy(ins[i], held[i], load_sem.at[i]) for i in range(count)]
    stores = [pltpu.make_async_copy(held[i], outs[i], store_sem.at[i]) for i in range(count)]
    for copy in loads:
        copy.start()
    for load, store in zip(loads, stores):
        load.wait()
        store.start()
    for copy in stores:
        copy.wait()


def body(query_vecs, key_vecs, value_vecs, out_grad, block_mask, norm_gain):
    n_ctx = lax.axis_size("ctx")
    n_head = lax.axis_size("head")
    rows, features = query_vecs.shape
    heads = features // D
    pairs = rows // PAIR
    ext = rows + 2 * RIM
    bf, f32 = jnp.bfloat16, jnp.float32
    dma = pltpu.SemaphoreType.DMA
    hbm = pl.BlockSpec(memory_space=pl.ANY)
    vmem = pl.BlockSpec(memory_space=pltpu.VMEM)
    fixed = pl.BlockSpec(memory_space=pltpu.HBM)
    big = jax.ShapeDtypeStruct((rows, features), bf)
    results = pl.pallas_call(
        functools.partial(kernel, n_ctx, n_head),
        out_shape=(big, big, big, big, jax.ShapeDtypeStruct((heads, D), f32)),
        in_specs=[fixed] * 6,
        out_specs=(hbm, hbm, hbm, hbm, vmem),
        scratch_shapes=[
            pltpu.VMEM(block_mask.shape, jnp.int32),
            pltpu.VMEM(norm_gain.shape, f32),
            pltpu.VMEM((rows, features), bf),
            pltpu.VMEM((heads, 2, ext, D), bf),
            pltpu.VMEM((rows, features), bf),
            pltpu.VMEM((8, 128), jnp.int32),
            pltpu.VMEM((8, 128), jnp.int32),
            pltpu.VMEM((2, pairs, WINDOW, PAIR), f32),
            pltpu.VMEM((heads, pairs, WINDOW, PAIR), f32),
            pltpu.VMEM((heads, pairs, WINDOW, PAIR), f32),
            pltpu.VMEM((rows, features), f32),
            pltpu.VMEM((rows, D), f32),
            pltpu.VMEM((rows, D), f32),
            pltpu.VMEM((n_head, 8, PAIR), f32),
            pltpu.VMEM((rows, D), f32),
            pltpu.VMEM((rows, D), f32),
            pltpu.VMEM((rows, features), bf),
            pltpu.VMEM((n_ctx, heads, D), f32),
            pltpu.VMEM((rows, features), bf),
            pltpu.VMEM((rows, features), bf),
            pltpu.VMEM((rows, features), f32),
            pltpu.VMEM((rows, features), f32),
            pltpu.VMEM((rows, features), bf),
            pltpu.VMEM((rows, features), bf),
            pltpu.VMEM((2, heads, 2, RIM, D), bf),
            pltpu.VMEM((2, heads, 2, RIM, D), bf),
            dma((4,)),
            dma((2, heads)),
            dma((2, heads)),
            dma,
            dma,
            dma((n_head,)),
            dma((n_head,)),
            dma((n_ctx,)),
            dma((n_ctx,)),
            dma((2, heads)),
            dma((2, heads)),
            dma((4,)),
            dma((2, heads)),
        ],
        compiler_params=pltpu.CompilerParams(
            collective_id=0, has_side_effects=True, vmem_limit_bytes=VMEM
        ),
        name="strand_attention",
    )(query_vecs, key_vecs, value_vecs, out_grad, block_mask, norm_gain)
    return pl.pallas_call(
        store_kernel,
        out_shape=tuple(jax.ShapeDtypeStruct(x.shape, x.dtype) for x in results),
        in_specs=[hbm] * 5,
        out_specs=(fixed,) * 5,
        scratch_shapes=[pltpu.VMEM(x.shape, x.dtype) for x in results] + [dma((5,)), dma((5,))],
        compiler_params=pltpu.CompilerParams(vmem_limit_bytes=VMEM),
        name="store_results",
    )(*results)


def solution(mesh):
    tokens = P("ctx", "head")
    return jax.shard_map(
        body,
        mesh=mesh,
        in_specs=(tokens, tokens, tokens, tokens, P("ctx", None), P("head", None)),
        out_specs=(tokens, tokens, tokens, tokens, P("head", None)),
        check_vma=False,
    )
```

```python
import functools
import math

import jax
import jax.numpy as jnp
from jax import lax
from jax.experimental import pallas as pl
from jax.experimental.pallas import tpu as pltpu
from jax.sharding import PartitionSpec as P

D = 128
BLOCK = 64
BAND = 2
RIM = BAND * BLOCK
PAIR = 2 * BLOCK
WINDOW = PAIR + 2 * RIM
VMEM = 64 * 1024 * 1024
GROUP = 2
MESH = pl.DeviceIdType.MESH
NT = (((1,), (1,)), ((), ()))
TN = (((0,), (0,)), ((), ()))
NN = (((1,), (0,)), ((), ()))


def dot(a, b, dims):
    return lax.dot_general(a, b, dims, preferred_element_type=jnp.float32)


def kernel(
    n_ctx, n_head,
    q_hbm, k_hbm, v_hbm, og_hbm, mask_hbm, gain_hbm,
    normed_hbm, dq_hbm, dk_hbm, dv_hbm, gg_ref,
    mask_ref, gain_ref, q, kvext, og, mine, theirs, bias, w1s, w2s, mixed, sq, inner, sall, invs, coefs,
    grad, gall, normed, dq, dk, dv, dko, dvo, out_halo, in_halo,
    load_sem, fsend, frecv, msend, mrecv, ssend, srecv, gsend, grecv, bsend, brecv, store_sem, kv_sem, relay, asend, rsend, rrecv,
):
    pos = lax.axis_index("ctx")
    me_h = lax.axis_index("head")
    rows, features = q.shape
    heads = features // D
    pairs = rows // PAIR
    blocks_dev = rows // BLOCK
    width = features * n_head
    scale = D ** -0.5
    last = n_ctx - 1

    small = [
        pltpu.make_async_copy(mask_hbm, mask_ref, load_sem.at[2]),
        pltpu.make_async_copy(gain_hbm, gain_ref, load_sem.at[3]),
    ]
    def cols(h):
        return pl.ds(pl.multiple_of(h * D, D), D)

    def head_load(kv, h):
        return pltpu.make_async_copy(
            (k_hbm, v_hbm)[kv].at[:, cols(h)], kvext.at[h, kv, pl.ds(RIM, rows)], kv_sem.at[kv, h]
        )

    loads = [
        pltpu.make_async_copy(q_hbm, q, load_sem.at[0]),
        pltpu.make_async_copy(og_hbm, og, load_sem.at[1]),
    ]
    kv_loads = [head_load(kv, h) for h in range(heads) for kv in range(2)]
    for copy in small + kv_loads + loads:
        copy.start()

    barrier = pltpu.get_barrier_semaphore()
    for o in range(1, n_ctx):
        pl.semaphore_signal(barrier, inc=1, device_id=(lax.rem(pos + o, n_ctx), me_h), device_id_type=MESH)
    for o in range(1, n_head):
        pl.semaphore_signal(barrier, inc=1, device_id=(pos, lax.rem(me_h + o, n_head)), device_id_type=MESH)
    mine[...] = jnp.zeros_like(mine)
    for copy in small:
        copy.wait()
    mine[0:blocks_dev, 0:mask_ref.shape[1]] = mask_ref[...]
    sall[me_h] = jnp.zeros(sall.shape[1:], jnp.float32)
    sq[...] = jnp.zeros_like(sq)
    inner[...] = jnp.zeros_like(inner)

    @pl.when(pos == 0)
    def _():
        kvext[:, :, 0:RIM, :] = jnp.zeros((heads, 2, RIM, D), kvext.dtype)

    @pl.when(pos == last)
    def _():
        kvext[:, :, rows + RIM :, :] = jnp.zeros((heads, 2, RIM, D), kvext.dtype)

    pl.semaphore_wait(barrier, n_ctx - 1 + n_head - 1)

    right = jnp.minimum(pos + 1, last)
    left = jnp.maximum(pos - 1, 0)

    def halo(way, h):
        from_row, to_row = ((rows, 0), (RIM, rows + RIM))[way]
        return pltpu.make_async_remote_copy(
            src_ref=kvext.at[h, :, pl.ds(from_row, RIM)],
            dst_ref=kvext.at[h, :, pl.ds(to_row, RIM)],
            send_sem=fsend.at[way, h],
            recv_sem=frecv.at[way, h],
            device_id=((right, left)[way], me_h),
            device_id_type=MESH,
        )

    mirror = pltpu.make_async_remote_copy(
        src_ref=mine, dst_ref=theirs, send_sem=msend, recv_sem=mrecv,
        device_id=(last - pos, me_h), device_id_type=MESH,
    )
    mirror.start()

    for copy in kv_loads:
        copy.wait()

    square = n_ctx == 8
    ends = (n_ctx // 2 - 1, n_ctx // 2)
    corners = (0, last)

    def first_leg(way, phase, step):
        h = step * GROUP + 1
        src = kvext.at[h, :, pl.ds((rows, RIM)[way], RIM)] if phase == 0 else out_halo.at[way, h]
        return pltpu.make_async_remote_copy(
            src_ref=src, dst_ref=relay.at[phase, step],
            send_sem=asend.at[phase, step], recv_sem=rrecv.at[phase, step],
            device_id=(corners[way], me_h), device_id_type=MESH,
        )

    def second_leg(way, phase, step):
        h = step * GROUP + 1
        if phase == 0:
            dst, sem = kvext.at[h, :, pl.ds((0, rows + RIM)[way], RIM)], frecv.at[way, h]
        else:
            dst, sem = in_halo.at[way, h], brecv.at[way, h]
        return pltpu.make_async_remote_copy(
            src_ref=relay.at[phase, step], dst_ref=dst,
            send_sem=rsend.at[phase, step], recv_sem=sem,
            device_id=(ends[1 - way], me_h), device_id_type=MESH,
        )

    def pass_on(phase, step):
        if square:
            for way in range(2):
                @pl.when(pos == corners[way])
                def _():
                    first_leg(way, phase, step).wait_recv()
                    second_leg(way, phase, step).start()

    def each_send(phase, step, plain, act):
        for i in range(GROUP):
            h = step * GROUP + i
            for way in range(2):
                able = (pos < last, pos > 0)[way]
                if square and i == 1:
                    @pl.when(pos == ends[way])
                    def _():
                        act(first_leg(way, phase, step))

                    able = able & (pos != ends[way])

                @pl.when(able)
                def _():
                    act(plain(way, h))

    def each_arrival(plain, h):
        @pl.when(pos > 0)
        def _():
            plain(0, h).wait_recv()

        @pl.when(pos < last)
        def _():
            plain(1, h).wait_recv()

    for step in range(heads // GROUP):
        each_send(0, step, halo, lambda copy: copy.start())
    mirror.wait_recv()

    all_blocks = blocks_dev * n_ctx
    row_block = lax.broadcasted_iota(jnp.int32, (WINDOW, PAIR), 0) // BLOCK
    second = lax.broadcasted_iota(jnp.int32, (8, PAIR), 1) >= BLOCK
    for strand in range(2):
        table = (mine, theirs)[strand]
        for p in range(pairs):
            first = pos * blocks_dev - BAND + 2 * p
            live = None
            for n in range(mask_ref.shape[1]):
                lists = []
                for b in (2 * p, 2 * p + 1):
                    r = b if strand == 0 else blocks_dev - 1 - b
                    lists.append(jnp.broadcast_to(table[r : r + 1, n : n + 1], (8, PAIR)))
                entry = jnp.where(second, lists[1], lists[0])
                if strand == 1:
                    target = all_blocks - 1 - entry
                else:
                    target = entry
                target = jnp.where(entry >= 0, target - first, -1)[0:1]
                hit = row_block == target
                live = hit if live is None else live | hit
            bias[strand, p] = jnp.where(live, 0.0, -1e30)

    for copy in loads:
        copy.wait()

    def forward(step, carry):
        group = [step * GROUP + i for i in range(GROUP)]
        pass_on(0, step)
        for h in group:
            each_arrival(halo, h)
        for p in range(pairs):
            r = pl.ds(p * PAIR, PAIR)
            w = pl.ds(p * PAIR, WINDOW)
            squares, products = sq[r, :], inner[r, :]
            for h in group:
                c = cols(h)
                scores = dot(kvext[h, 0, w], q[r, c], NT) * scale
                total = None
                for strand, kept in ((0, w1s), (1, w2s)):
                    s = scores + bias[strand, p]
                    e = jnp.exp(s - jnp.max(s, axis=0, keepdims=True))
                    e = e * (1.0 / jnp.sum(e, axis=0, keepdims=True))
                    kept[h, p] = e
                    total = e if total is None else total + e
                m = dot(total.astype(jnp.bfloat16), kvext[h, 1, w], TN)
                mixed[r, c] = m
                squares = squares + m * m
                products = products + gain_ref[pl.ds(h, 1), :] * og[r, c].astype(jnp.float32) * m
            sq[r, :] = squares
            inner[r, :] = products
        return carry

    lax.fori_loop(0, heads // GROUP, forward, 0)

    for p in range(pairs):
        r = slice(p * PAIR, (p + 1) * PAIR)
        sall[me_h, p : p + 1, :] = jnp.sum(sq[r, :].T, axis=0, keepdims=True)
        sall[me_h, pairs + p : pairs + p + 1, :] = jnp.sum(inner[r, :].T, axis=0, keepdims=True)

    def stat(slot, o, to):
        return pltpu.make_async_remote_copy(
            src_ref=sall.at[slot], dst_ref=sall.at[slot],
            send_sem=ssend.at[o], recv_sem=srecv.at[slot],
            device_id=(pos, to), device_id_type=MESH,
        )

    for o in range(1, n_head):
        stat(me_h, o, lax.rem(me_h + o, n_head)).start()
    for o in range(1, n_head):
        stat(lax.rem(me_h + o, n_head), o, me_h).wait_recv()
    tot = sall[0]
    for s in range(1, n_head):
        tot = tot + sall[s]
    inv = 1.0 / jnp.sqrt(tot[0:pairs] / width + 1e-06)
    coef = tot[pairs : 2 * pairs] / width * (inv * inv * inv)
    for p in range(pairs):
        r = slice(p * PAIR, (p + 1) * PAIR)
        invs[r, :] = jnp.broadcast_to(inv[p : p + 1], (PAIR, D)).T
        coefs[r, :] = jnp.broadcast_to(coef[p : p + 1], (PAIR, D)).T

    def normalise(h, carry):
        c = cols(h)
        gain = gain_ref[pl.ds(h, 1), :]
        m = mixed[:, c]
        g = og[:, c].astype(jnp.float32)
        iv = invs[...]
        mi = m * iv
        normed[:, c] = (gain * mi).astype(jnp.bfloat16)
        grad[:, c] = (gain * g * iv - m * coefs[...]).astype(jnp.bfloat16)
        gall[pos, pl.ds(h, 1), :] = jnp.sum(g * mi, axis=0, keepdims=True)
        return carry

    lax.fori_loop(0, heads, normalise, 0)

    def share(slot, o, to):
        return pltpu.make_async_remote_copy(
            src_ref=gall.at[slot], dst_ref=gall.at[slot],
            send_sem=gsend.at[o], recv_sem=grecv.at[slot],
            device_id=(to, me_h), device_id_type=MESH,
        )

    for o in range(1, n_ctx):
        share(pos, o, lax.rem(pos + o, n_ctx)).start()
    out_copies = [pltpu.make_async_copy(normed, normed_hbm, store_sem.at[0])]
    out_copies[0].start()

    def back(way, h):
        return pltpu.make_async_remote_copy(
            src_ref=out_halo.at[way, h],
            dst_ref=in_halo.at[way, h],
            send_sem=bsend.at[way, h],
            recv_sem=brecv.at[way, h],
            device_id=((right, left)[way], me_h),
            device_id_type=MESH,
        )

    def backward(step, carry):
        group = [step * GROUP + i for i in range(GROUP)]
        for h in group:
            c = cols(h)
            parts = []
            for p in range(pairs):
                r = pl.ds(p * PAIR, PAIR)
                w = pl.ds(p * PAIR, WINDOW)
                g = grad[r, c]
                w1, w2 = w1s[h, p], w2s[h, p]
                wg = dot(kvext[h, 1, w], g, NT)
                c1 = jnp.sum(w1 * wg, axis=0, keepdims=True)
                c2 = jnp.sum(w2 * wg, axis=0, keepdims=True)
                ds = ((w1 * (wg - c1) + w2 * (wg - c2)) * scale).astype(jnp.bfloat16)
                dvw = dot((w1 + w2).astype(jnp.bfloat16), g, NN)
                dkw = dot(ds, q[r, c], NN)
                dq[r, c] = dot(ds, kvext[h, 0, w], TN).astype(jnp.bfloat16)
                parts.append((dkw, dvw))
            for kv, own in ((0, dk), (1, dv)):
                out_halo[1, h, kv] = parts[0][kv][0:RIM].astype(jnp.bfloat16)
                out_halo[0, h, kv] = parts[-1][kv][WINDOW - RIM :].astype(jnp.bfloat16)
                for p in range(pairs):
                    mid = parts[p][kv][RIM : RIM + PAIR]
                    if p > 0:
                        mid = mid + parts[p - 1][kv][RIM + PAIR :]
                    if p < pairs - 1:
                        mid = mid + parts[p + 1][kv][0:RIM]
                    own[pl.ds(p * PAIR, PAIR), c] = mid
        each_send(1, step, back, lambda copy: copy.start())

        @pl.when(step > 0)
        def _():
            pass_on(1, step - 1)

        return carry

    lax.fori_loop(0, heads // GROUP, backward, 0)
    pass_on(1, heads // GROUP - 1)
    dq_copy = pltpu.make_async_copy(dq, dq_hbm, store_sem.at[1])
    dq_copy.start()
    out_copies.append(dq_copy)

    for o in range(1, n_ctx):
        share(lax.rem(pos + o, n_ctx), o, pos).wait_recv()
    total = gall[0]
    for s in range(1, n_ctx):
        total = total + gall[s]
    gg_ref[...] = total / math.sqrt(rows * n_ctx)

    @pl.when(pos == 0)
    def _():
        in_halo[0] = jnp.zeros(in_halo.shape[1:], in_halo.dtype)

    @pl.when(pos == last)
    def _():
        in_halo[1] = jnp.zeros(in_halo.shape[1:], in_halo.dtype)

    def settle(h, carry):
        c = cols(h)
        each_arrival(back, h)
        for kv, own, out in ((0, dk, dko), (1, dv, dvo)):
            out[0:RIM, c] = (own[0:RIM, c] + in_halo[0, h, kv].astype(jnp.float32)).astype(jnp.bfloat16)
            out[rows - RIM : rows, c] = (
                own[rows - RIM : rows, c] + in_halo[1, h, kv].astype(jnp.float32)
            ).astype(jnp.bfloat16)
        return carry

    lax.fori_loop(0, heads, settle, 0)
    for i, (src, dst) in enumerate(((dko, dk_hbm), (dvo, dv_hbm))):
        copy = pltpu.make_async_copy(src, dst, store_sem.at[2 + i])
        copy.start()
        out_copies.append(copy)

    mirror.wait_send()
    for o in range(1, n_head):
        stat(me_h, o, lax.rem(me_h + o, n_head)).wait_send()
    for o in range(1, n_ctx):
        share(pos, o, lax.rem(pos + o, n_ctx)).wait_send()

    for step in range(heads // GROUP):
        for phase, plain in ((0, halo), (1, back)):
            each_send(phase, step, plain, lambda copy: copy.wait_send())
            if square:
                for way in range(2):
                    @pl.when(pos == corners[way])
                    def _():
                        second_leg(way, phase, step).wait_send()
    for copy in out_copies:
        copy.wait()


def store_kernel(*refs):
    count = (len(refs) - 2) // 3
    ins, outs, held = refs[:count], refs[count : 2 * count], refs[2 * count : 3 * count]
    load_sem, store_sem = refs[3 * count :]
    loads = [pltpu.make_async_copy(ins[i], held[i], load_sem.at[i]) for i in range(count)]
    stores = [pltpu.make_async_copy(held[i], outs[i], store_sem.at[i]) for i in range(count)]
    for copy in loads:
        copy.start()
    for load, store in zip(loads, stores):
        load.wait()
        store.start()
    for copy in stores:
        copy.wait()


def body(query_vecs, key_vecs, value_vecs, out_grad, block_mask, norm_gain):
    n_ctx = lax.axis_size("ctx")
    n_head = lax.axis_size("head")
    rows, features = query_vecs.shape
    heads = features // D
    pairs = rows // PAIR
    ext = rows + 2 * RIM
    bf, f32 = jnp.bfloat16, jnp.float32
    dma = pltpu.SemaphoreType.DMA
    hbm = pl.BlockSpec(memory_space=pl.ANY)
    vmem = pl.BlockSpec(memory_space=pltpu.VMEM)
    fixed = pl.BlockSpec(memory_space=pltpu.HBM)
    big = jax.ShapeDtypeStruct((rows, features), bf)
    results = pl.pallas_call(
        functools.partial(kernel, n_ctx, n_head),
        out_shape=(big, big, big, big, jax.ShapeDtypeStruct((heads, D), f32)),
        in_specs=[fixed] * 6,
        out_specs=(hbm, hbm, hbm, hbm, vmem),
        scratch_shapes=[
            pltpu.VMEM(block_mask.shape, jnp.int32),
            pltpu.VMEM(norm_gain.shape, f32),
            pltpu.VMEM((rows, features), bf),
            pltpu.VMEM((heads, 2, ext, D), bf),
            pltpu.VMEM((rows, features), bf),
            pltpu.VMEM((8, 128), jnp.int32),
            pltpu.VMEM((8, 128), jnp.int32),
            pltpu.VMEM((2, pairs, WINDOW, PAIR), f32),
            pltpu.VMEM((heads, pairs, WINDOW, PAIR), f32),
            pltpu.VMEM((heads, pairs, WINDOW, PAIR), f32),
            pltpu.VMEM((rows, features), f32),
            pltpu.VMEM((rows, D), f32),
            pltpu.VMEM((rows, D), f32),
            pltpu.VMEM((n_head, 8, PAIR), f32),
            pltpu.VMEM((rows, D), f32),
            pltpu.VMEM((rows, D), f32),
            pltpu.VMEM((rows, features), bf),
            pltpu.VMEM((n_ctx, heads, D), f32),
            pltpu.VMEM((rows, features), bf),
            pltpu.VMEM((rows, features), bf),
            pltpu.VMEM((rows, features), f32),
            pltpu.VMEM((rows, features), f32),
            pltpu.VMEM((rows, features), bf),
            pltpu.VMEM((rows, features), bf),
            pltpu.VMEM((2, heads, 2, RIM, D), bf),
            pltpu.VMEM((2, heads, 2, RIM, D), bf),
            dma((4,)),
            dma((2, heads)),
            dma((2, heads)),
            dma,
            dma,
            dma((n_head,)),
            dma((n_head,)),
            dma((n_ctx,)),
            dma((n_ctx,)),
            dma((2, heads)),
            dma((2, heads)),
            dma((4,)),
            dma((2, heads)),
            pltpu.VMEM((2, heads // GROUP, 2, RIM, D), bf),
            dma((2, heads // GROUP)),
            dma((2, heads // GROUP)),
            dma((2, heads // GROUP)),
        ],
        compiler_params=pltpu.CompilerParams(
            collective_id=0, has_side_effects=True, vmem_limit_bytes=VMEM
        ),
        name="strand_attention",
    )(query_vecs, key_vecs, value_vecs, out_grad, block_mask, norm_gain)
    return pl.pallas_call(
        store_kernel,
        out_shape=tuple(jax.ShapeDtypeStruct(x.shape, x.dtype) for x in results),
        in_specs=[hbm] * 5,
        out_specs=(fixed,) * 5,
        scratch_shapes=[pltpu.VMEM(x.shape, x.dtype) for x in results] + [dma((5,)), dma((5,))],
        compiler_params=pltpu.CompilerParams(vmem_limit_bytes=VMEM),
        name="store_results",
    )(*results)


def solution(mesh):
    tokens = P("ctx", "head")
    return jax.shard_map(
        body,
        mesh=mesh,
        in_specs=(tokens, tokens, tokens, tokens, P("ctx", None), P("head", None)),
        out_specs=(tokens, tokens, tokens, tokens, P("head", None)),
        check_vma=False,
    )
```

```python
import functools
import math

import jax
import jax.numpy as jnp
from jax import lax
from jax.experimental import pallas as pl
from jax.experimental.pallas import tpu as pltpu
from jax.sharding import PartitionSpec as P

D = 128
BLOCK = 64
BAND = 2
RIM = BAND * BLOCK
PAIR = 2 * BLOCK
WINDOW = PAIR + 2 * RIM
VMEM = 64 * 1024 * 1024
GROUP = 2
MESH = pl.DeviceIdType.MESH
NT = (((1,), (1,)), ((), ()))
TN = (((0,), (0,)), ((), ()))
NN = (((1,), (0,)), ((), ()))


def dot(a, b, dims):
    return lax.dot_general(a, b, dims, preferred_element_type=jnp.float32)


def kernel(
    n_ctx, n_head,
    q_hbm, k_hbm, v_hbm, og_hbm, mask_hbm, gain_hbm,
    normed_hbm, dq_hbm, dk_hbm, dv_hbm, gg_ref,
    mask_ref, gain_ref, q, kvext, og, mine, theirs, bias, w1s, w2s, mixed, sq, inner, sall, invs, coefs,
    grad, gall, normed, dq, dk, dv, dko, dvo, out_halo, in_halo,
    load_sem, fsend, frecv, msend, mrecv, ssend, srecv, gsend, grecv, bsend, brecv, store_sem, kv_sem, relay, asend, rsend, rrecv,
):
    pos = lax.axis_index("ctx")
    me_h = lax.axis_index("head")
    rows, features = q.shape
    heads = features // D
    pairs = rows // PAIR
    blocks_dev = rows // BLOCK
    width = features * n_head
    scale = D ** -0.5
    last = n_ctx - 1

    small = [
        pltpu.make_async_copy(mask_hbm, mask_ref, load_sem.at[2]),
        pltpu.make_async_copy(gain_hbm, gain_ref, load_sem.at[3]),
    ]
    def cols(h):
        return pl.ds(pl.multiple_of(h * D, D), D)

    def head_load(kv, h):
        return pltpu.make_async_copy(
            (k_hbm, v_hbm)[kv].at[:, cols(h)], kvext.at[h, kv, pl.ds(RIM, rows)], kv_sem.at[kv, h]
        )

    loads = [
        pltpu.make_async_copy(q_hbm, q, load_sem.at[0]),
        pltpu.make_async_copy(og_hbm, og, load_sem.at[1]),
    ]
    kv_loads = [head_load(kv, h) for h in range(heads) for kv in range(2)]
    for copy in small + kv_loads + loads:
        copy.start()

    barrier = pltpu.get_barrier_semaphore()
    for o in range(1, n_ctx):
        pl.semaphore_signal(barrier, inc=1, device_id=(lax.rem(pos + o, n_ctx), me_h), device_id_type=MESH)
    for o in range(1, n_head):
        pl.semaphore_signal(barrier, inc=1, device_id=(pos, lax.rem(me_h + o, n_head)), device_id_type=MESH)
    mine[...] = jnp.zeros_like(mine)
    for copy in small:
        copy.wait()
    mine[0:blocks_dev, 0:mask_ref.shape[1]] = mask_ref[...]
    sall[me_h] = jnp.zeros(sall.shape[1:], jnp.float32)
    sq[...] = jnp.zeros_like(sq)
    inner[...] = jnp.zeros_like(inner)

    @pl.when(pos == 0)
    def _():
        kvext[:, :, 0:RIM, :] = jnp.zeros((heads, 2, RIM, D), kvext.dtype)

    @pl.when(pos == last)
    def _():
        kvext[:, :, rows + RIM :, :] = jnp.zeros((heads, 2, RIM, D), kvext.dtype)

    pl.semaphore_wait(barrier, n_ctx - 1 + n_head - 1)

    right = jnp.minimum(pos + 1, last)
    left = jnp.maximum(pos - 1, 0)

    def halo(way, h):
        from_row, to_row = ((rows, 0), (RIM, rows + RIM))[way]
        return pltpu.make_async_remote_copy(
            src_ref=kvext.at[h, :, pl.ds(from_row, RIM)],
            dst_ref=kvext.at[h, :, pl.ds(to_row, RIM)],
            send_sem=fsend.at[way, h],
            recv_sem=frecv.at[way, h],
            device_id=((right, left)[way], me_h),
            device_id_type=MESH,
        )

    mirror = pltpu.make_async_remote_copy(
        src_ref=mine, dst_ref=theirs, send_sem=msend, recv_sem=mrecv,
        device_id=(last - pos, me_h), device_id_type=MESH,
    )
    mirror.start()

    for copy in kv_loads:
        copy.wait()

    square = n_ctx == 8
    ends = (n_ctx // 2 - 1, n_ctx // 2)
    corners = (last, 0)
    half = heads // 2

    def first_leg(way, phase, j):
        h = half + j if phase == 0 else j
        src = kvext.at[h, :, pl.ds((rows, RIM)[way], RIM)] if phase == 0 else out_halo.at[way, h]
        return pltpu.make_async_remote_copy(
            src_ref=src, dst_ref=relay.at[phase, j],
            send_sem=asend.at[phase, j], recv_sem=rrecv.at[phase, j],
            device_id=(corners[way], me_h), device_id_type=MESH,
        )

    def second_leg(way, phase, j):
        h = half + j if phase == 0 else j
        if phase == 0:
            dst, sem = kvext.at[h, :, pl.ds((0, rows + RIM)[way], RIM)], frecv.at[way, h]
        else:
            dst, sem = in_halo.at[way, h], brecv.at[way, h]
        return pltpu.make_async_remote_copy(
            src_ref=relay.at[phase, j], dst_ref=dst,
            send_sem=rsend.at[phase, j], recv_sem=sem,
            device_id=(ends[1 - way], me_h), device_id_type=MESH,
        )

    def pass_on(phase, j):
        if square:
            for way in range(2):
                @pl.when(pos == corners[way])
                def _():
                    first_leg(way, phase, j).wait_recv()
                    second_leg(way, phase, j).start()

    def each_detour(phase, j, act):
        if square:
            for way in range(2):
                @pl.when(pos == ends[way])
                def _():
                    act(first_leg(way, phase, j))

    def each_direct(phase, h, plain, act):
        detoured = (h >= half) if phase == 0 else (h < half)
        for way in range(2):
            able = (pos < last, pos > 0)[way]
            if square:
                able = able & jnp.logical_not((pos == ends[way]) & detoured)

            @pl.when(able)
            def _():
                act(plain(way, h))

    def each_arrival(plain, h):
        @pl.when(pos > 0)
        def _():
            plain(0, h).wait_recv()

        @pl.when(pos < last)
        def _():
            plain(1, h).wait_recv()

    for h in range(heads):
        if h < half:
            each_detour(0, h, lambda copy: copy.start())
        each_direct(0, h, halo, lambda copy: copy.start())
    mirror.wait_recv()

    all_blocks = blocks_dev * n_ctx
    row_block = lax.broadcasted_iota(jnp.int32, (WINDOW, PAIR), 0) // BLOCK
    second = lax.broadcasted_iota(jnp.int32, (8, PAIR), 1) >= BLOCK
    for strand in range(2):
        table = (mine, theirs)[strand]
        for p in range(pairs):
            first = pos * blocks_dev - BAND + 2 * p
            live = None
            for n in range(mask_ref.shape[1]):
                lists = []
                for b in (2 * p, 2 * p + 1):
                    r = b if strand == 0 else blocks_dev - 1 - b
                    lists.append(jnp.broadcast_to(table[r : r + 1, n : n + 1], (8, PAIR)))
                entry = jnp.where(second, lists[1], lists[0])
                if strand == 1:
                    target = all_blocks - 1 - entry
                else:
                    target = entry
                target = jnp.where(entry >= 0, target - first, -1)[0:1]
                hit = row_block == target
                live = hit if live is None else live | hit
            bias[strand, p] = jnp.where(live, 0.0, -1e30)

    for copy in loads:
        copy.wait()

    def forward(step, carry):
        group = [step * GROUP + i for i in range(GROUP)]
        for i in range(GROUP):
            j = step * GROUP + i

            @pl.when(j < half)
            def _():
                pass_on(0, j)

        for h in group:
            each_arrival(halo, h)
        for p in range(pairs):
            r = pl.ds(p * PAIR, PAIR)
            w = pl.ds(p * PAIR, WINDOW)
            squares, products = sq[r, :], inner[r, :]
            for h in group:
                c = cols(h)
                scores = dot(kvext[h, 0, w], q[r, c], NT) * scale
                total = None
                for strand, kept in ((0, w1s), (1, w2s)):
                    s = scores + bias[strand, p]
                    e = jnp.exp(s - jnp.max(s, axis=0, keepdims=True))
                    e = e * (1.0 / jnp.sum(e, axis=0, keepdims=True))
                    kept[h, p] = e
                    total = e if total is None else total + e
                m = dot(total.astype(jnp.bfloat16), kvext[h, 1, w], TN)
                mixed[r, c] = m
                squares = squares + m * m
                products = products + gain_ref[pl.ds(h, 1), :] * og[r, c].astype(jnp.float32) * m
            sq[r, :] = squares
            inner[r, :] = products
        return carry

    lax.fori_loop(0, heads // GROUP, forward, 0)

    for p in range(pairs):
        r = slice(p * PAIR, (p + 1) * PAIR)
        sall[me_h, p : p + 1, :] = jnp.sum(sq[r, :].T, axis=0, keepdims=True)
        sall[me_h, pairs + p : pairs + p + 1, :] = jnp.sum(inner[r, :].T, axis=0, keepdims=True)

    def stat(slot, o, to):
        return pltpu.make_async_remote_copy(
            src_ref=sall.at[slot], dst_ref=sall.at[slot],
            send_sem=ssend.at[o], recv_sem=srecv.at[slot],
            device_id=(pos, to), device_id_type=MESH,
        )

    for o in range(1, n_head):
        stat(me_h, o, lax.rem(me_h + o, n_head)).start()
    for o in range(1, n_head):
        stat(lax.rem(me_h + o, n_head), o, me_h).wait_recv()
    tot = sall[0]
    for s in range(1, n_head):
        tot = tot + sall[s]
    inv = 1.0 / jnp.sqrt(tot[0:pairs] / width + 1e-06)
    coef = tot[pairs : 2 * pairs] / width * (inv * inv * inv)
    for p in range(pairs):
        r = slice(p * PAIR, (p + 1) * PAIR)
        invs[r, :] = jnp.broadcast_to(inv[p : p + 1], (PAIR, D)).T
        coefs[r, :] = jnp.broadcast_to(coef[p : p + 1], (PAIR, D)).T

    def normalise(h, carry):
        c = cols(h)
        gain = gain_ref[pl.ds(h, 1), :]
        m = mixed[:, c]
        g = og[:, c].astype(jnp.float32)
        iv = invs[...]
        mi = m * iv
        normed[:, c] = (gain * mi).astype(jnp.bfloat16)
        grad[:, c] = (gain * g * iv - m * coefs[...]).astype(jnp.bfloat16)
        gall[pos, pl.ds(h, 1), :] = jnp.sum(g * mi, axis=0, keepdims=True)
        return carry

    lax.fori_loop(0, heads, normalise, 0)

    def share(slot, o, to):
        return pltpu.make_async_remote_copy(
            src_ref=gall.at[slot], dst_ref=gall.at[slot],
            send_sem=gsend.at[o], recv_sem=grecv.at[slot],
            device_id=(to, me_h), device_id_type=MESH,
        )

    for o in range(1, n_ctx):
        share(pos, o, lax.rem(pos + o, n_ctx)).start()
    out_copies = [pltpu.make_async_copy(normed, normed_hbm, store_sem.at[0])]
    out_copies[0].start()

    def back(way, h):
        return pltpu.make_async_remote_copy(
            src_ref=out_halo.at[way, h],
            dst_ref=in_halo.at[way, h],
            send_sem=bsend.at[way, h],
            recv_sem=brecv.at[way, h],
            device_id=((right, left)[way], me_h),
            device_id_type=MESH,
        )

    def backward(step, carry):
        group = [step * GROUP + i for i in range(GROUP)]
        for h in group:
            c = cols(h)
            parts = []
            for p in range(pairs):
                r = pl.ds(p * PAIR, PAIR)
                w = pl.ds(p * PAIR, WINDOW)
                g = grad[r, c]
                w1, w2 = w1s[h, p], w2s[h, p]
                wg = dot(kvext[h, 1, w], g, NT)
                c1 = jnp.sum(w1 * wg, axis=0, keepdims=True)
                c2 = jnp.sum(w2 * wg, axis=0, keepdims=True)
                ds = ((w1 * (wg - c1) + w2 * (wg - c2)) * scale).astype(jnp.bfloat16)
                dvw = dot((w1 + w2).astype(jnp.bfloat16), g, NN)
                dkw = dot(ds, q[r, c], NN)
                dq[r, c] = dot(ds, kvext[h, 0, w], TN).astype(jnp.bfloat16)
                parts.append((dkw, dvw))
            for kv, own in ((0, dk), (1, dv)):
                out_halo[1, h, kv] = parts[0][kv][0:RIM].astype(jnp.bfloat16)
                out_halo[0, h, kv] = parts[-1][kv][WINDOW - RIM :].astype(jnp.bfloat16)
                for p in range(pairs):
                    mid = parts[p][kv][RIM : RIM + PAIR]
                    if p > 0:
                        mid = mid + parts[p - 1][kv][RIM + PAIR :]
                    if p < pairs - 1:
                        mid = mid + parts[p + 1][kv][0:RIM]
                    own[pl.ds(p * PAIR, PAIR), c] = mid
        for h in group:
            @pl.when(h < half)
            def _():
                each_detour(1, h, lambda copy: copy.start())

            each_direct(1, h, back, lambda copy: copy.start())

        for h in group:
            @pl.when((h >= GROUP) & (h < half + GROUP))
            def _():
                pass_on(1, h - GROUP)

        return carry

    lax.fori_loop(0, heads // GROUP, backward, 0)
    dq_copy = pltpu.make_async_copy(dq, dq_hbm, store_sem.at[1])
    dq_copy.start()
    out_copies.append(dq_copy)

    for o in range(1, n_ctx):
        share(lax.rem(pos + o, n_ctx), o, pos).wait_recv()
    total = gall[0]
    for s in range(1, n_ctx):
        total = total + gall[s]
    gg_ref[...] = total / math.sqrt(rows * n_ctx)

    @pl.when(pos == 0)
    def _():
        in_halo[0] = jnp.zeros(in_halo.shape[1:], in_halo.dtype)

    @pl.when(pos == last)
    def _():
        in_halo[1] = jnp.zeros(in_halo.shape[1:], in_halo.dtype)

    def settle(h, carry):
        c = cols(h)
        each_arrival(back, h)
        for kv, own, out in ((0, dk, dko), (1, dv, dvo)):
            out[0:RIM, c] = (own[0:RIM, c] + in_halo[0, h, kv].astype(jnp.float32)).astype(jnp.bfloat16)
            out[rows - RIM : rows, c] = (
                own[rows - RIM : rows, c] + in_halo[1, h, kv].astype(jnp.float32)
            ).astype(jnp.bfloat16)
        return carry

    lax.fori_loop(0, heads, settle, 0)
    for i, (src, dst) in enumerate(((dko, dk_hbm), (dvo, dv_hbm))):
        copy = pltpu.make_async_copy(src, dst, store_sem.at[2 + i])
        copy.start()
        out_copies.append(copy)

    mirror.wait_send()
    for o in range(1, n_head):
        stat(me_h, o, lax.rem(me_h + o, n_head)).wait_send()
    for o in range(1, n_ctx):
        share(pos, o, lax.rem(pos + o, n_ctx)).wait_send()

    for phase, plain in ((0, halo), (1, back)):
        for h in range(heads):
            each_direct(phase, h, plain, lambda copy: copy.wait_send())
        for j in range(half):
            each_detour(phase, j, lambda copy: copy.wait_send())
            if square:
                for way in range(2):
                    @pl.when(pos == corners[way])
                    def _():
                        second_leg(way, phase, j).wait_send()
    for copy in out_copies:
        copy.wait()


def store_kernel(*refs):
    count = (len(refs) - 2) // 3
    ins, outs, held = refs[:count], refs[count : 2 * count], refs[2 * count : 3 * count]
    load_sem, store_sem = refs[3 * count :]
    loads = [pltpu.make_async_copy(ins[i], held[i], load_sem.at[i]) for i in range(count)]
    stores = [pltpu.make_async_copy(held[i], outs[i], store_sem.at[i]) for i in range(count)]
    for copy in loads:
        copy.start()
    for load, store in zip(loads, stores):
        load.wait()
        store.start()
    for copy in stores:
        copy.wait()


def body(query_vecs, key_vecs, value_vecs, out_grad, block_mask, norm_gain):
    n_ctx = lax.axis_size("ctx")
    n_head = lax.axis_size("head")
    rows, features = query_vecs.shape
    heads = features // D
    pairs = rows // PAIR
    ext = rows + 2 * RIM
    bf, f32 = jnp.bfloat16, jnp.float32
    dma = pltpu.SemaphoreType.DMA
    hbm = pl.BlockSpec(memory_space=pl.ANY)
    vmem = pl.BlockSpec(memory_space=pltpu.VMEM)
    fixed = pl.BlockSpec(memory_space=pltpu.HBM)
    big = jax.ShapeDtypeStruct((rows, features), bf)
    results = pl.pallas_call(
        functools.partial(kernel, n_ctx, n_head),
        out_shape=(big, big, big, big, jax.ShapeDtypeStruct((heads, D), f32)),
        in_specs=[fixed] * 6,
        out_specs=(hbm, hbm, hbm, hbm, vmem),
        scratch_shapes=[
            pltpu.VMEM(block_mask.shape, jnp.int32),
            pltpu.VMEM(norm_gain.shape, f32),
            pltpu.VMEM((rows, features), bf),
            pltpu.VMEM((heads, 2, ext, D), bf),
            pltpu.VMEM((rows, features), bf),
            pltpu.VMEM((8, 128), jnp.int32),
            pltpu.VMEM((8, 128), jnp.int32),
            pltpu.VMEM((2, pairs, WINDOW, PAIR), f32),
            pltpu.VMEM((heads, pairs, WINDOW, PAIR), f32),
            pltpu.VMEM((heads, pairs, WINDOW, PAIR), f32),
            pltpu.VMEM((rows, features), f32),
            pltpu.VMEM((rows, D), f32),
            pltpu.VMEM((rows, D), f32),
            pltpu.VMEM((n_head, 8, PAIR), f32),
            pltpu.VMEM((rows, D), f32),
            pltpu.VMEM((rows, D), f32),
            pltpu.VMEM((rows, features), bf),
            pltpu.VMEM((n_ctx, heads, D), f32),
            pltpu.VMEM((rows, features), bf),
            pltpu.VMEM((rows, features), bf),
            pltpu.VMEM((rows, features), f32),
            pltpu.VMEM((rows, features), f32),
            pltpu.VMEM((rows, features), bf),
            pltpu.VMEM((rows, features), bf),
            pltpu.VMEM((2, heads, 2, RIM, D), bf),
            pltpu.VMEM((2, heads, 2, RIM, D), bf),
            dma((4,)),
            dma((2, heads)),
            dma((2, heads)),
            dma,
            dma,
            dma((n_head,)),
            dma((n_head,)),
            dma((n_ctx,)),
            dma((n_ctx,)),
            dma((2, heads)),
            dma((2, heads)),
            dma((4,)),
            dma((2, heads)),
            pltpu.VMEM((2, heads // 2, 2, RIM, D), bf),
            dma((2, heads // 2)),
            dma((2, heads // 2)),
            dma((2, heads // 2)),
        ],
        compiler_params=pltpu.CompilerParams(
            collective_id=0, has_side_effects=True, vmem_limit_bytes=VMEM
        ),
        name="strand_attention",
    )(query_vecs, key_vecs, value_vecs, out_grad, block_mask, norm_gain)
    return pl.pallas_call(
        store_kernel,
        out_shape=tuple(jax.ShapeDtypeStruct(x.shape, x.dtype) for x in results),
        in_specs=[hbm] * 5,
        out_specs=(fixed,) * 5,
        scratch_shapes=[pltpu.VMEM(x.shape, x.dtype) for x in results] + [dma((5,)), dma((5,))],
        compiler_params=pltpu.CompilerParams(vmem_limit_bytes=VMEM),
        name="store_results",
    )(*results)


def solution(mesh):
    tokens = P("ctx", "head")
    return jax.shard_map(
        body,
        mesh=mesh,
        in_specs=(tokens, tokens, tokens, tokens, P("ctx", None), P("head", None)),
        out_specs=(tokens, tokens, tokens, tokens, P("head", None)),
        check_vma=False,
    )
```

```python
import functools
import math

import jax
import jax.numpy as jnp
from jax import lax
from jax.experimental import pallas as pl
from jax.experimental.pallas import tpu as pltpu
from jax.sharding import PartitionSpec as P

D = 128
BLOCK = 64
BAND = 2
RIM = BAND * BLOCK
PAIR = 2 * BLOCK
WINDOW = PAIR + 2 * RIM
VMEM = 64 * 1024 * 1024
GROUP = 1
MESH = pl.DeviceIdType.MESH
NT = (((1,), (1,)), ((), ()))
TN = (((0,), (0,)), ((), ()))
NN = (((1,), (0,)), ((), ()))


def dot(a, b, dims):
    return lax.dot_general(a, b, dims, preferred_element_type=jnp.float32)


def kernel(
    n_ctx, n_head,
    q_hbm, k_hbm, v_hbm, og_hbm, mask_hbm, gain_hbm,
    normed_hbm, dq_hbm, dk_hbm, dv_hbm, gg_ref,
    mask_ref, gain_ref, q, kvext, og, mine, theirs, bias, w1s, w2s, wsum, mixed, sq, inner, sall, invs, coefs,
    grad, gall, normed, dq, dk, dv, dko, dvo, out_halo, in_halo,
    load_sem, fsend, frecv, msend, mrecv, ssend, srecv, gsend, grecv, bsend, brecv, store_sem, kv_sem, out_sem,
):
    pos = lax.axis_index("ctx")
    me_h = lax.axis_index("head")
    rows, features = q.shape
    heads = features // D
    pairs = rows // PAIR
    blocks_dev = rows // BLOCK
    width = features * n_head
    scale = D ** -0.5
    last = n_ctx - 1

    small = [
        pltpu.make_async_copy(mask_hbm, mask_ref, load_sem.at[2]),
        pltpu.make_async_copy(gain_hbm, gain_ref, load_sem.at[3]),
    ]
    def cols(h):
        return pl.ds(pl.multiple_of(h * D, D), D)

    def head_load(kv, h):
        return pltpu.make_async_copy(
            (k_hbm, v_hbm)[kv].at[:, cols(h)], kvext.at[h, kv, pl.ds(RIM, rows)], kv_sem.at[kv, h]
        )

    loads = [
        pltpu.make_async_copy(q_hbm, q, load_sem.at[0]),
        pltpu.make_async_copy(og_hbm, og, load_sem.at[1]),
    ]
    kv_loads = [head_load(kv, h) for h in range(heads) for kv in range(2)]
    for copy in small + kv_loads + loads:
        copy.start()

    barrier = pltpu.get_barrier_semaphore()
    for o in range(1, n_ctx):
        pl.semaphore_signal(barrier, inc=1, device_id=(lax.rem(pos + o, n_ctx), me_h), device_id_type=MESH)
    for o in range(1, n_head):
        pl.semaphore_signal(barrier, inc=1, device_id=(pos, lax.rem(me_h + o, n_head)), device_id_type=MESH)
    mine[...] = jnp.zeros_like(mine)
    for copy in small:
        copy.wait()
    mine[0:blocks_dev, 0:mask_ref.shape[1]] = mask_ref[...]
    sall[me_h] = jnp.zeros(sall.shape[1:], jnp.float32)
    sq[...] = jnp.zeros_like(sq)
    inner[...] = jnp.zeros_like(inner)

    @pl.when(pos == 0)
    def _():
        kvext[:, :, 0:RIM, :] = jnp.zeros((heads, 2, RIM, D), kvext.dtype)

    @pl.when(pos == last)
    def _():
        kvext[:, :, rows + RIM :, :] = jnp.zeros((heads, 2, RIM, D), kvext.dtype)

    pl.semaphore_wait(barrier, n_ctx - 1 + n_head - 1)

    right = jnp.minimum(pos + 1, last)
    left = jnp.maximum(pos - 1, 0)

    def halo(way, h):
        from_row, to_row = ((rows, 0), (RIM, rows + RIM))[way]
        return pltpu.make_async_remote_copy(
            src_ref=kvext.at[h, :, pl.ds(from_row, RIM)],
            dst_ref=kvext.at[h, :, pl.ds(to_row, RIM)],
            send_sem=fsend.at[way, h],
            recv_sem=frecv.at[way, h],
            device_id=((right, left)[way], me_h),
            device_id_type=MESH,
        )

    mirror = pltpu.make_async_remote_copy(
        src_ref=mine, dst_ref=theirs, send_sem=msend, recv_sem=mrecv,
        device_id=(last - pos, me_h), device_id_type=MESH,
    )
    mirror.start()

    for copy in kv_loads:
        copy.wait()

    def each_way(act, plain, h):
        @pl.when(pos < last)
        def _():
            act(plain(0, h))

        @pl.when(pos > 0)
        def _():
            act(plain(1, h))

    def each_arrival(plain, h):
        @pl.when(pos > 0)
        def _():
            plain(0, h).wait_recv()

        @pl.when(pos < last)
        def _():
            plain(1, h).wait_recv()

    for h in range(heads):
        each_way(lambda copy: copy.start(), halo, h)
    mirror.wait_recv()

    all_blocks = blocks_dev * n_ctx
    row_block = lax.broadcasted_iota(jnp.int32, (WINDOW, PAIR), 0) // BLOCK
    second = lax.broadcasted_iota(jnp.int32, (8, PAIR), 1) >= BLOCK
    for strand in range(2):
        table = (mine, theirs)[strand]
        for p in range(pairs):
            first = pos * blocks_dev - BAND + 2 * p
            live = None
            for n in range(mask_ref.shape[1]):
                lists = []
                for b in (2 * p, 2 * p + 1):
                    r = b if strand == 0 else blocks_dev - 1 - b
                    lists.append(jnp.broadcast_to(table[r : r + 1, n : n + 1], (8, PAIR)))
                entry = jnp.where(second, lists[1], lists[0])
                if strand == 1:
                    target = all_blocks - 1 - entry
                else:
                    target = entry
                target = jnp.where(entry >= 0, target - first, -1)[0:1]
                hit = row_block == target
                live = hit if live is None else live | hit
            bias[strand, p] = jnp.where(live, 0.0, -1e30)

    for copy in loads:
        copy.wait()

    def forward(step, carry):
        group = [step * GROUP + i for i in range(GROUP)]
        for h in group:
            each_arrival(halo, h)
        for p in range(pairs):
            r = pl.ds(p * PAIR, PAIR)
            w = pl.ds(p * PAIR, WINDOW)
            squares, products = sq[r, :], inner[r, :]
            for h in group:
                c = cols(h)
                scores = dot(kvext[h, 0, w], q[r, c], NT) * scale
                total = None
                for strand, kept in ((0, w1s), (1, w2s)):
                    s = scores + bias[strand, p]
                    e = jnp.exp(s - jnp.max(s, axis=0, keepdims=True))
                    e = e * (1.0 / jnp.sum(e, axis=0, keepdims=True))
                    kept[h, p] = e
                    total = e if total is None else total + e
                both = total.astype(jnp.bfloat16)
                wsum[h, p] = both
                m = dot(both, kvext[h, 1, w], TN)
                mixed[r, c] = m
                squares = squares + m * m
                products = products + gain_ref[pl.ds(h, 1), :] * og[r, c].astype(jnp.float32) * m
            sq[r, :] = squares
            inner[r, :] = products
        return carry

    lax.fori_loop(0, heads // GROUP, forward, 0)

    for p in range(pairs):
        r = slice(p * PAIR, (p + 1) * PAIR)
        sall[me_h, p : p + 1, :] = jnp.sum(sq[r, :].T, axis=0, keepdims=True)
        sall[me_h, pairs + p : pairs + p + 1, :] = jnp.sum(inner[r, :].T, axis=0, keepdims=True)

    def stat(slot, o, to):
        return pltpu.make_async_remote_copy(
            src_ref=sall.at[slot], dst_ref=sall.at[slot],
            send_sem=ssend.at[o], recv_sem=srecv.at[slot],
            device_id=(pos, to), device_id_type=MESH,
        )

    for o in range(1, n_head):
        stat(me_h, o, lax.rem(me_h + o, n_head)).start()
    for o in range(1, n_head):
        stat(lax.rem(me_h + o, n_head), o, me_h).wait_recv()
    tot = sall[0]
    for s in range(1, n_head):
        tot = tot + sall[s]
    inv = 1.0 / jnp.sqrt(tot[0:pairs] / width + 1e-06)
    coef = tot[pairs : 2 * pairs] / width * (inv * inv * inv)
    for p in range(pairs):
        r = slice(p * PAIR, (p + 1) * PAIR)
        invs[r, :] = jnp.broadcast_to(inv[p : p + 1], (PAIR, D)).T
        coefs[r, :] = jnp.broadcast_to(coef[p : p + 1], (PAIR, D)).T

    def normalise(h, carry):
        c = cols(h)
        gain = gain_ref[pl.ds(h, 1), :]
        m = mixed[:, c]
        g = og[:, c].astype(jnp.float32)
        iv = invs[...]
        mi = m * iv
        normed[:, c] = (gain * mi).astype(jnp.bfloat16)
        grad[:, c] = (gain * g * iv - m * coefs[...]).astype(jnp.bfloat16)
        gall[pos, pl.ds(h, 1), :] = jnp.sum(g * mi, axis=0, keepdims=True)
        return carry

    lax.fori_loop(0, heads, normalise, 0)

    def share(slot, o, to):
        return pltpu.make_async_remote_copy(
            src_ref=gall.at[slot], dst_ref=gall.at[slot],
            send_sem=gsend.at[o], recv_sem=grecv.at[slot],
            device_id=(to, me_h), device_id_type=MESH,
        )

    for o in range(1, n_ctx):
        share(pos, o, lax.rem(pos + o, n_ctx)).start()
    out_copies = [pltpu.make_async_copy(normed, normed_hbm, store_sem.at[0])]
    out_copies[0].start()

    def back(way, h):
        return pltpu.make_async_remote_copy(
            src_ref=out_halo.at[way, h],
            dst_ref=in_halo.at[way, h],
            send_sem=bsend.at[way, h],
            recv_sem=brecv.at[way, h],
            device_id=((right, left)[way], me_h),
            device_id_type=MESH,
        )

    def backward(step, carry):
        group = [step * GROUP + i for i in range(GROUP)]
        for h in group:
            c = cols(h)
            parts = []
            for p in range(pairs):
                r = pl.ds(p * PAIR, PAIR)
                w = pl.ds(p * PAIR, WINDOW)
                g = grad[r, c]
                w1, w2 = w1s[h, p], w2s[h, p]
                wg = dot(kvext[h, 1, w], g, NT)
                c1 = jnp.sum(w1 * wg, axis=0, keepdims=True)
                c2 = jnp.sum(w2 * wg, axis=0, keepdims=True)
                ds = ((w1 * (wg - c1) + w2 * (wg - c2)) * scale).astype(jnp.bfloat16)
                dvw = dot(wsum[h, p], g, NN)
                dkw = dot(ds, q[r, c], NN)
                dq[r, c] = dot(ds, kvext[h, 0, w], TN).astype(jnp.bfloat16)
                parts.append((dkw, dvw))
            for kv, own in ((0, dk), (1, dv)):
                out_halo[1, h, kv] = parts[0][kv][0:RIM].astype(jnp.bfloat16)
                out_halo[0, h, kv] = parts[-1][kv][WINDOW - RIM :].astype(jnp.bfloat16)
                for p in range(pairs):
                    mid = parts[p][kv][RIM : RIM + PAIR]
                    if p > 0:
                        mid = mid + parts[p - 1][kv][RIM + PAIR :]
                    if p < pairs - 1:
                        mid = mid + parts[p + 1][kv][0:RIM]
                    own[pl.ds(p * PAIR, PAIR), c] = mid
        for h in group:
            each_way(lambda copy: copy.start(), back, h)
        return carry

    lax.fori_loop(0, heads // GROUP, backward, 0)
    dq_copy = pltpu.make_async_copy(dq, dq_hbm, store_sem.at[1])
    dq_copy.start()
    out_copies.append(dq_copy)

    for o in range(1, n_ctx):
        share(lax.rem(pos + o, n_ctx), o, pos).wait_recv()
    total = gall[0]
    for s in range(1, n_ctx):
        total = total + gall[s]
    gg_ref[...] = total / math.sqrt(rows * n_ctx)

    @pl.when(pos == 0)
    def _():
        in_halo[0] = jnp.zeros(in_halo.shape[1:], in_halo.dtype)

    @pl.when(pos == last)
    def _():
        in_halo[1] = jnp.zeros(in_halo.shape[1:], in_halo.dtype)

    def result(i, h):
        return pltpu.make_async_copy(
            (dko, dvo)[i].at[:, cols(h)], (dk_hbm, dv_hbm)[i].at[:, cols(h)], out_sem.at[i, h]
        )

    def settle(h, carry):
        c = cols(h)
        each_arrival(back, h)
        for kv, own, out in ((0, dk, dko), (1, dv, dvo)):
            out[0:RIM, c] = (own[0:RIM, c] + in_halo[0, h, kv].astype(jnp.float32)).astype(jnp.bfloat16)
            out[rows - RIM : rows, c] = (
                own[rows - RIM : rows, c] + in_halo[1, h, kv].astype(jnp.float32)
            ).astype(jnp.bfloat16)
        for i in range(2):
            result(i, h).start()
        return carry

    lax.fori_loop(0, heads, settle, 0)
    for h in range(heads):
        out_copies.extend(result(i, h) for i in range(2))

    mirror.wait_send()
    for o in range(1, n_head):
        stat(me_h, o, lax.rem(me_h + o, n_head)).wait_send()
    for o in range(1, n_ctx):
        share(pos, o, lax.rem(pos + o, n_ctx)).wait_send()

    for h in range(heads):
        each_way(lambda copy: copy.wait_send(), halo, h)
        each_way(lambda copy: copy.wait_send(), back, h)
    for copy in out_copies:
        copy.wait()


def store_kernel(*refs):
    count = (len(refs) - 2) // 3
    ins, outs, held = refs[:count], refs[count : 2 * count], refs[2 * count : 3 * count]
    load_sem, store_sem = refs[3 * count :]
    loads = [pltpu.make_async_copy(ins[i], held[i], load_sem.at[i]) for i in range(count)]
    stores = [pltpu.make_async_copy(held[i], outs[i], store_sem.at[i]) for i in range(count)]
    for copy in loads:
        copy.start()
    for load, store in zip(loads, stores):
        load.wait()
        store.start()
    for copy in stores:
        copy.wait()


def body(query_vecs, key_vecs, value_vecs, out_grad, block_mask, norm_gain):
    n_ctx = lax.axis_size("ctx")
    n_head = lax.axis_size("head")
    rows, features = query_vecs.shape
    heads = features // D
    pairs = rows // PAIR
    ext = rows + 2 * RIM
    bf, f32 = jnp.bfloat16, jnp.float32
    dma = pltpu.SemaphoreType.DMA
    hbm = pl.BlockSpec(memory_space=pl.ANY)
    vmem = pl.BlockSpec(memory_space=pltpu.VMEM)
    fixed = pl.BlockSpec(memory_space=pltpu.HBM)
    big = jax.ShapeDtypeStruct((rows, features), bf)
    results = pl.pallas_call(
        functools.partial(kernel, n_ctx, n_head),
        out_shape=(big, big, big, big, jax.ShapeDtypeStruct((heads, D), f32)),
        in_specs=[fixed] * 6,
        out_specs=(hbm, hbm, hbm, hbm, vmem),
        scratch_shapes=[
            pltpu.VMEM(block_mask.shape, jnp.int32),
            pltpu.VMEM(norm_gain.shape, f32),
            pltpu.VMEM((rows, features), bf),
            pltpu.VMEM((heads, 2, ext, D), bf),
            pltpu.VMEM((rows, features), bf),
            pltpu.VMEM((8, 128), jnp.int32),
            pltpu.VMEM((8, 128), jnp.int32),
            pltpu.VMEM((2, pairs, WINDOW, PAIR), f32),
            pltpu.VMEM((heads, pairs, WINDOW, PAIR), f32),
            pltpu.VMEM((heads, pairs, WINDOW, PAIR), f32),
            pltpu.VMEM((heads, pairs, WINDOW, PAIR), bf),
            pltpu.VMEM((rows, features), f32),
            pltpu.VMEM((rows, D), f32),
            pltpu.VMEM((rows, D), f32),
            pltpu.VMEM((n_head, 8, PAIR), f32),
            pltpu.VMEM((rows, D), f32),
            pltpu.VMEM((rows, D), f32),
            pltpu.VMEM((rows, features), bf),
            pltpu.VMEM((n_ctx, heads, D), f32),
            pltpu.VMEM((rows, features), bf),
            pltpu.VMEM((rows, features), bf),
            pltpu.VMEM((rows, features), f32),
            pltpu.VMEM((rows, features), f32),
            pltpu.VMEM((rows, features), bf),
            pltpu.VMEM((rows, features), bf),
            pltpu.VMEM((2, heads, 2, RIM, D), bf),
            pltpu.VMEM((2, heads, 2, RIM, D), bf),
            dma((4,)),
            dma((2, heads)),
            dma((2, heads)),
            dma,
            dma,
            dma((n_head,)),
            dma((n_head,)),
            dma((n_ctx,)),
            dma((n_ctx,)),
            dma((2, heads)),
            dma((2, heads)),
            dma((4,)),
            dma((2, heads)),
            dma((2, heads)),
        ],
        compiler_params=pltpu.CompilerParams(
            collective_id=0, has_side_effects=True, vmem_limit_bytes=VMEM
        ),
        name="strand_attention",
    )(query_vecs, key_vecs, value_vecs, out_grad, block_mask, norm_gain)
    return pl.pallas_call(
        store_kernel,
        out_shape=tuple(jax.ShapeDtypeStruct(x.shape, x.dtype) for x in results),
        in_specs=[hbm] * 5,
        out_specs=(fixed,) * 5,
        scratch_shapes=[pltpu.VMEM(x.shape, x.dtype) for x in results] + [dma((5,)), dma((5,))],
        compiler_params=pltpu.CompilerParams(vmem_limit_bytes=VMEM),
        name="store_results",
    )(*results)


def solution(mesh):
    tokens = P("ctx", "head")
    return jax.shard_map(
        body,
        mesh=mesh,
        in_specs=(tokens, tokens, tokens, tokens, P("ctx", None), P("head", None)),
        out_specs=(tokens, tokens, tokens, tokens, P("head", None)),
        check_vma=False,
    )
```

```python
import functools
import math

import jax
import jax.numpy as jnp
from jax import lax
from jax.experimental import pallas as pl
from jax.experimental.pallas import tpu as pltpu
from jax.sharding import PartitionSpec as P

D = 128
BLOCK = 64
BAND = 2
RIM = BAND * BLOCK
PAIR = 2 * BLOCK
WINDOW = PAIR + 2 * RIM
VMEM = 64 * 1024 * 1024
GROUP = 1
MESH = pl.DeviceIdType.MESH
NT = (((1,), (1,)), ((), ()))
TN = (((0,), (0,)), ((), ()))
NN = (((1,), (0,)), ((), ()))


def dot(a, b, dims):
    return lax.dot_general(a, b, dims, preferred_element_type=jnp.float32)


def kernel(
    n_ctx, n_head,
    q_hbm, k_hbm, v_hbm, og_hbm, mask_hbm, gain_hbm,
    normed_hbm, dq_hbm, dk_hbm, dv_hbm, gg_ref,
    mask_ref, gain_ref, q, kvext, og, mine, theirs, bias, w1s, w2s, wsum, mixed, sq, inner, sall, invs, coefs,
    grad, gall, normed, dq, dk, dv, dko, dvo, out_halo, in_halo,
    load_sem, fsend, frecv, msend, mrecv, ssend, srecv, gsend, grecv, bsend, brecv, store_sem, kv_sem, out_sem,
):
    pos = lax.axis_index("ctx")
    me_h = lax.axis_index("head")
    rows, features = q.shape
    heads = features // D
    pairs = rows // PAIR
    blocks_dev = rows // BLOCK
    width = features * n_head
    scale = D ** -0.5
    last = n_ctx - 1

    small = [
        pltpu.make_async_copy(mask_hbm, mask_ref, load_sem.at[2]),
        pltpu.make_async_copy(gain_hbm, gain_ref, load_sem.at[3]),
    ]
    def cols(h):
        return pl.ds(pl.multiple_of(h * D, D), D)

    def head_load(kv, h):
        return pltpu.make_async_copy(
            (k_hbm, v_hbm)[kv].at[:, cols(h)], kvext.at[h, kv, pl.ds(RIM, rows)], kv_sem.at[kv, h]
        )

    loads = [
        pltpu.make_async_copy(q_hbm, q, load_sem.at[0]),
        pltpu.make_async_copy(og_hbm, og, load_sem.at[1]),
    ]
    kv_loads = [head_load(kv, h) for h in range(heads) for kv in range(2)]
    for copy in small + kv_loads + loads:
        copy.start()

    barrier = pltpu.get_barrier_semaphore()
    for o in range(1, n_ctx):
        pl.semaphore_signal(barrier, inc=1, device_id=(lax.rem(pos + o, n_ctx), me_h), device_id_type=MESH)
    for o in range(1, n_head):
        pl.semaphore_signal(barrier, inc=1, device_id=(pos, lax.rem(me_h + o, n_head)), device_id_type=MESH)
    mine[...] = jnp.zeros_like(mine)
    for copy in small:
        copy.wait()
    mine[0:blocks_dev, 0:mask_ref.shape[1]] = mask_ref[...]
    sall[me_h] = jnp.zeros(sall.shape[1:], jnp.float32)
    sq[...] = jnp.zeros_like(sq)
    inner[...] = jnp.zeros_like(inner)

    @pl.when(pos == 0)
    def _():
        kvext[:, :, 0:RIM, :] = jnp.zeros((heads, 2, RIM, D), kvext.dtype)

    @pl.when(pos == last)
    def _():
        kvext[:, :, rows + RIM :, :] = jnp.zeros((heads, 2, RIM, D), kvext.dtype)

    pl.semaphore_wait(barrier, n_ctx - 1 + n_head - 1)

    right = jnp.minimum(pos + 1, last)
    left = jnp.maximum(pos - 1, 0)

    def halo(way, h):
        from_row, to_row = ((rows, 0), (RIM, rows + RIM))[way]
        return pltpu.make_async_remote_copy(
            src_ref=kvext.at[h, :, pl.ds(from_row, RIM)],
            dst_ref=kvext.at[h, :, pl.ds(to_row, RIM)],
            send_sem=fsend.at[way, h],
            recv_sem=frecv.at[way, h],
            device_id=((right, left)[way], me_h),
            device_id_type=MESH,
        )

    mirror = pltpu.make_async_remote_copy(
        src_ref=mine, dst_ref=theirs, send_sem=msend, recv_sem=mrecv,
        device_id=(last - pos, me_h), device_id_type=MESH,
    )
    mirror.start()


    def each_way(act, plain, h):
        @pl.when(pos < last)
        def _():
            act(plain(0, h))

        @pl.when(pos > 0)
        def _():
            act(plain(1, h))

    def each_arrival(plain, h):
        @pl.when(pos > 0)
        def _():
            plain(0, h).wait_recv()

        @pl.when(pos < last)
        def _():
            plain(1, h).wait_recv()

    for h in range(heads):
        kv_loads[2 * h].wait()
        kv_loads[2 * h + 1].wait()
        each_way(lambda copy: copy.start(), halo, h)
    mirror.wait_recv()

    all_blocks = blocks_dev * n_ctx
    row_block = lax.broadcasted_iota(jnp.int32, (WINDOW, PAIR), 0) // BLOCK
    second = lax.broadcasted_iota(jnp.int32, (8, PAIR), 1) >= BLOCK
    for strand in range(2):
        table = (mine, theirs)[strand]
        for p in range(pairs):
            first = pos * blocks_dev - BAND + 2 * p
            live = None
            for n in range(mask_ref.shape[1]):
                lists = []
                for b in (2 * p, 2 * p + 1):
                    r = b if strand == 0 else blocks_dev - 1 - b
                    lists.append(jnp.broadcast_to(table[r : r + 1, n : n + 1], (8, PAIR)))
                entry = jnp.where(second, lists[1], lists[0])
                if strand == 1:
                    target = all_blocks - 1 - entry
                else:
                    target = entry
                target = jnp.where(entry >= 0, target - first, -1)[0:1]
                hit = row_block == target
                live = hit if live is None else live | hit
            bias[strand, p] = jnp.where(live, 0.0, -1e30)

    for copy in loads:
        copy.wait()

    def forward(step, carry):
        group = [step * GROUP + i for i in range(GROUP)]
        for h in group:
            each_arrival(halo, h)
        for p in range(pairs):
            r = pl.ds(p * PAIR, PAIR)
            w = pl.ds(p * PAIR, WINDOW)
            squares, products = sq[r, :], inner[r, :]
            for h in group:
                c = cols(h)
                scores = dot(kvext[h, 0, w], q[r, c], NT) * scale
                total = None
                for strand, kept in ((0, w1s), (1, w2s)):
                    s = scores + bias[strand, p]
                    e = jnp.exp(s - jnp.max(s, axis=0, keepdims=True))
                    e = e * (1.0 / jnp.sum(e, axis=0, keepdims=True))
                    kept[h, p] = e
                    total = e if total is None else total + e
                both = total.astype(jnp.bfloat16)
                wsum[h, p] = both
                m = dot(both, kvext[h, 1, w], TN)
                mixed[r, c] = m
                squares = squares + m * m
                products = products + gain_ref[pl.ds(h, 1), :] * og[r, c].astype(jnp.float32) * m
            sq[r, :] = squares
            inner[r, :] = products
        return carry

    lax.fori_loop(0, heads // GROUP, forward, 0)

    for p in range(pairs):
        r = slice(p * PAIR, (p + 1) * PAIR)
        sall[me_h, p : p + 1, :] = jnp.sum(sq[r, :].T, axis=0, keepdims=True)
        sall[me_h, pairs + p : pairs + p + 1, :] = jnp.sum(inner[r, :].T, axis=0, keepdims=True)

    def stat(slot, o, to):
        return pltpu.make_async_remote_copy(
            src_ref=sall.at[slot], dst_ref=sall.at[slot],
            send_sem=ssend.at[o], recv_sem=srecv.at[slot],
            device_id=(pos, to), device_id_type=MESH,
        )

    for o in range(1, n_head):
        stat(me_h, o, lax.rem(me_h + o, n_head)).start()
    for o in range(1, n_head):
        stat(lax.rem(me_h + o, n_head), o, me_h).wait_recv()
    tot = sall[0]
    for s in range(1, n_head):
        tot = tot + sall[s]
    inv = 1.0 / jnp.sqrt(tot[0:pairs] / width + 1e-06)
    coef = tot[pairs : 2 * pairs] / width * (inv * inv * inv)
    for p in range(pairs):
        r = slice(p * PAIR, (p + 1) * PAIR)
        invs[r, :] = jnp.broadcast_to(inv[p : p + 1], (PAIR, D)).T
        coefs[r, :] = jnp.broadcast_to(coef[p : p + 1], (PAIR, D)).T

    def normalise(h, carry):
        c = cols(h)
        gain = gain_ref[pl.ds(h, 1), :]
        m = mixed[:, c]
        g = og[:, c].astype(jnp.float32)
        iv = invs[...]
        mi = m * iv
        normed[:, c] = (gain * mi).astype(jnp.bfloat16)
        grad[:, c] = (gain * g * iv - m * coefs[...]).astype(jnp.bfloat16)
        gall[pos, pl.ds(h, 1), :] = jnp.sum(g * mi, axis=0, keepdims=True)
        return carry

    lax.fori_loop(0, heads, normalise, 0)

    def share(slot, o, to):
        return pltpu.make_async_remote_copy(
            src_ref=gall.at[slot], dst_ref=gall.at[slot],
            send_sem=gsend.at[o], recv_sem=grecv.at[slot],
            device_id=(to, me_h), device_id_type=MESH,
        )

    for o in range(1, n_ctx):
        share(pos, o, lax.rem(pos + o, n_ctx)).start()
    out_copies = [pltpu.make_async_copy(normed, normed_hbm, store_sem.at[0])]
    out_copies[0].start()

    def back(way, h):
        return pltpu.make_async_remote_copy(
            src_ref=out_halo.at[way, h],
            dst_ref=in_halo.at[way, h],
            send_sem=bsend.at[way, h],
            recv_sem=brecv.at[way, h],
            device_id=((right, left)[way], me_h),
            device_id_type=MESH,
        )

    def backward(step, carry):
        group = [step * GROUP + i for i in range(GROUP)]
        for h in group:
            c = cols(h)
            parts = []
            for p in range(pairs):
                r = pl.ds(p * PAIR, PAIR)
                w = pl.ds(p * PAIR, WINDOW)
                g = grad[r, c]
                w1, w2 = w1s[h, p], w2s[h, p]
                wg = dot(kvext[h, 1, w], g, NT)
                c1 = jnp.sum(w1 * wg, axis=0, keepdims=True)
                c2 = jnp.sum(w2 * wg, axis=0, keepdims=True)
                ds = ((w1 * (wg - c1) + w2 * (wg - c2)) * scale).astype(jnp.bfloat16)
                dvw = dot(wsum[h, p], g, NN)
                dkw = dot(ds, q[r, c], NN)
                dq[r, c] = dot(ds, kvext[h, 0, w], TN).astype(jnp.bfloat16)
                parts.append((dkw, dvw))
            for kv, own in ((0, dk), (1, dv)):
                out_halo[1, h, kv] = parts[0][kv][0:RIM].astype(jnp.bfloat16)
                out_halo[0, h, kv] = parts[-1][kv][WINDOW - RIM :].astype(jnp.bfloat16)
                for p in range(pairs):
                    mid = parts[p][kv][RIM : RIM + PAIR]
                    if p > 0:
                        mid = mid + parts[p - 1][kv][RIM + PAIR :]
                    if p < pairs - 1:
                        mid = mid + parts[p + 1][kv][0:RIM]
                    own[pl.ds(p * PAIR, PAIR), c] = mid
        for h in group:
            each_way(lambda copy: copy.start(), back, h)
        return carry

    lax.fori_loop(0, heads // GROUP, backward, 0)
    dq_copy = pltpu.make_async_copy(dq, dq_hbm, store_sem.at[1])
    dq_copy.start()
    out_copies.append(dq_copy)

    for o in range(1, n_ctx):
        share(lax.rem(pos + o, n_ctx), o, pos).wait_recv()
    total = gall[0]
    for s in range(1, n_ctx):
        total = total + gall[s]
    gg_ref[...] = total / math.sqrt(rows * n_ctx)

    @pl.when(pos == 0)
    def _():
        in_halo[0] = jnp.zeros(in_halo.shape[1:], in_halo.dtype)

    @pl.when(pos == last)
    def _():
        in_halo[1] = jnp.zeros(in_halo.shape[1:], in_halo.dtype)

    def result(i, h):
        return pltpu.make_async_copy(
            (dko, dvo)[i].at[:, cols(h)], (dk_hbm, dv_hbm)[i].at[:, cols(h)], out_sem.at[i, h]
        )

    def settle(h, carry):
        c = cols(h)
        each_arrival(back, h)
        for kv, own, out in ((0, dk, dko), (1, dv, dvo)):
            out[0:RIM, c] = (own[0:RIM, c] + in_halo[0, h, kv].astype(jnp.float32)).astype(jnp.bfloat16)
            out[rows - RIM : rows, c] = (
                own[rows - RIM : rows, c] + in_halo[1, h, kv].astype(jnp.float32)
            ).astype(jnp.bfloat16)
        for i in range(2):
            result(i, h).start()
        return carry

    lax.fori_loop(0, heads, settle, 0)
    for h in range(heads):
        out_copies.extend(result(i, h) for i in range(2))

    mirror.wait_send()
    for o in range(1, n_head):
        stat(me_h, o, lax.rem(me_h + o, n_head)).wait_send()
    for o in range(1, n_ctx):
        share(pos, o, lax.rem(pos + o, n_ctx)).wait_send()

    for h in range(heads):
        each_way(lambda copy: copy.wait_send(), halo, h)
        each_way(lambda copy: copy.wait_send(), back, h)
    for copy in out_copies:
        copy.wait()


def store_kernel(*refs):
    count = (len(refs) - 2) // 3
    ins, outs, held = refs[:count], refs[count : 2 * count], refs[2 * count : 3 * count]
    load_sem, store_sem = refs[3 * count :]
    loads = [pltpu.make_async_copy(ins[i], held[i], load_sem.at[i]) for i in range(count)]
    stores = [pltpu.make_async_copy(held[i], outs[i], store_sem.at[i]) for i in range(count)]
    for copy in loads:
        copy.start()
    for load, store in zip(loads, stores):
        load.wait()
        store.start()
    for copy in stores:
        copy.wait()


def body(query_vecs, key_vecs, value_vecs, out_grad, block_mask, norm_gain):
    n_ctx = lax.axis_size("ctx")
    n_head = lax.axis_size("head")
    rows, features = query_vecs.shape
    heads = features // D
    pairs = rows // PAIR
    ext = rows + 2 * RIM
    bf, f32 = jnp.bfloat16, jnp.float32
    dma = pltpu.SemaphoreType.DMA
    hbm = pl.BlockSpec(memory_space=pl.ANY)
    vmem = pl.BlockSpec(memory_space=pltpu.VMEM)
    fixed = pl.BlockSpec(memory_space=pltpu.HBM)
    big = jax.ShapeDtypeStruct((rows, features), bf)
    results = pl.pallas_call(
        functools.partial(kernel, n_ctx, n_head),
        out_shape=(big, big, big, big, jax.ShapeDtypeStruct((heads, D), f32)),
        in_specs=[fixed] * 6,
        out_specs=(hbm, hbm, hbm, hbm, vmem),
        scratch_shapes=[
            pltpu.VMEM(block_mask.shape, jnp.int32),
            pltpu.VMEM(norm_gain.shape, f32),
            pltpu.VMEM((rows, features), bf),
            pltpu.VMEM((heads, 2, ext, D), bf),
            pltpu.VMEM((rows, features), bf),
            pltpu.VMEM((8, 128), jnp.int32),
            pltpu.VMEM((8, 128), jnp.int32),
            pltpu.VMEM((2, pairs, WINDOW, PAIR), f32),
            pltpu.VMEM((heads, pairs, WINDOW, PAIR), f32),
            pltpu.VMEM((heads, pairs, WINDOW, PAIR), f32),
            pltpu.VMEM((heads, pairs, WINDOW, PAIR), bf),
            pltpu.VMEM((rows, features), f32),
            pltpu.VMEM((rows, D), f32),
            pltpu.VMEM((rows, D), f32),
            pltpu.VMEM((n_head, 8, PAIR), f32),
            pltpu.VMEM((rows, D), f32),
            pltpu.VMEM((rows, D), f32),
            pltpu.VMEM((rows, features), bf),
            pltpu.VMEM((n_ctx, heads, D), f32),
            pltpu.VMEM((rows, features), bf),
            pltpu.VMEM((rows, features), bf),
            pltpu.VMEM((rows, features), f32),
            pltpu.VMEM((rows, features), f32),
            pltpu.VMEM((rows, features), bf),
            pltpu.VMEM((rows, features), bf),
            pltpu.VMEM((2, heads, 2, RIM, D), bf),
            pltpu.VMEM((2, heads, 2, RIM, D), bf),
            dma((4,)),
            dma((2, heads)),
            dma((2, heads)),
            dma,
            dma,
            dma((n_head,)),
            dma((n_head,)),
            dma((n_ctx,)),
            dma((n_ctx,)),
            dma((2, heads)),
            dma((2, heads)),
            dma((4,)),
            dma((2, heads)),
            dma((2, heads)),
        ],
        compiler_params=pltpu.CompilerParams(
            collective_id=0, has_side_effects=True, vmem_limit_bytes=VMEM
        ),
        name="strand_attention",
    )(query_vecs, key_vecs, value_vecs, out_grad, block_mask, norm_gain)
    return pl.pallas_call(
        store_kernel,
        out_shape=tuple(jax.ShapeDtypeStruct(x.shape, x.dtype) for x in results),
        in_specs=[hbm] * 5,
        out_specs=(fixed,) * 5,
        scratch_shapes=[pltpu.VMEM(x.shape, x.dtype) for x in results] + [dma((5,)), dma((5,))],
        compiler_params=pltpu.CompilerParams(vmem_limit_bytes=VMEM),
        name="store_results",
    )(*results)


def solution(mesh):
    tokens = P("ctx", "head")
    return jax.shard_map(
        body,
        mesh=mesh,
        in_specs=(tokens, tokens, tokens, tokens, P("ctx", None), P("head", None)),
        out_specs=(tokens, tokens, tokens, tokens, P("head", None)),
        check_vma=False,
    )
```
